32 devices in a mesh: sub: 8 (over z, x), grp: 4 (over y, core).
Axes of the slice: x: 2, y: 2, z: 4, core: 2. Of those that a mesh axis runs over, the one named last changes fastest.
Arguments:
- flexibility: bfloat16 [8, 4, 512, 512], P('sub', 'grp'), as said below
- dirichlet_schur: bfloat16 [8, 4, 512, 512], P('sub', 'grp'), as said below
- subdomain_loads: bfloat16 [8, 4, 512, 128], P('sub', 'grp'), may hold values from -6 to 6
- coupling: bfloat16 [8, 4, 512, 24], P('sub', 'grp'), may hold values from -0.25 to 0.25
- coarse_rows: bfloat16 [8, 4, 24, 2048], P('sub', 'grp'), as said below
- neighbors: int32 [8, 4, 6], P('sub', 'grp'), may hold values from 0 to 7, as said below
- interface_rows: int32 [8, 4, 6, 16], P('sub', 'grp'), may hold values from 0 to 511, as said below
- coarse_map: int32 [8, 4, 24], P('sub', 'grp'), may hold values from 0 to 2047, as said below
Outputs:
- solution: float32 [8, 4, 512, 128], P('sub', 'grp')
- preconditioned: float32 [8, 4, 512, 128], P('sub', 'grp')
The draws below stay inside these ranges and needn't reach their ends.
Inputs may be any that keep to these rules, and one draw needn't show every extreme that they name: `neighbors`: each subdomain lists 6 distinct sub indices other than its own, of subdomains with the same grp index; if subdomain (i, g) lists j, then (j, g) lists i. `interface_rows`: the 6 x 16 rows of one subdomain are distinct; the j-th row that s lists for neighbor t and the j-th row that t lists for s are the same interface point. `coarse_map`: the 24 entries of one subdomain are distinct. coarse_rows of subdomain s are the rows coarse_map of s of one symmetric positive definite matrix of order 2048. `flexibility`: each subdomain's block is symmetric positive definite. `dirichlet_schur`: each subdomain's block is symmetric positive definite.
All inputs are finite; a program needn't handle non-finite values.
Results may differ from the reference program's by a relative error of at most 0.0084.
Values may be sent and summed in bfloat16 or wider, within the bound.
No kernel may reach another device: no remote copies, remote signals or barrier semaphores. Data moves between devices by JAX's collectives and lax.ppermute only.
A program may use at most 64 MiB of HBM per device.

```python
import jax
import jax.numpy as jnp
from jax import lax

ORDER = 512
COARSE = 2048
COLUMNS = 128
CORNERS = 24
ROWS_EACH = 16
ITERATIONS = 1
NEIGHBORS = 6
N_SUB = 8
N_GRP = 4


def spd_blocks(key, matrix_order):
    block_count = N_SUB * N_GRP
    inner_rank = matrix_order // 4

    def single(block_key):
        diag_key, fact_key = jax.random.split(block_key, 2)
        diagonal = jnp.exp(jax.random.uniform(diag_key, (matrix_order,), jnp.float32, jnp.log(0.5), jnp.log(2.0)))
        factor = jax.random.normal(fact_key, (matrix_order, inner_rank), jnp.float32) * jnp.sqrt(0.6 / inner_rank)
        product = jnp.dot(factor, factor.T, precision=lax.Precision.HIGHEST)
        matrix = jnp.diag(diagonal) + 0.5 * (product + product.T)
        return matrix
    blocks = lax.map(single, jax.random.split(key, block_count))
    return blocks.reshape(N_SUB, N_GRP, matrix_order, matrix_order)


def subset_rows(key, total_size, pick_count):
    block_count = N_SUB * N_GRP
    key_list = jax.random.split(key, block_count)

    def select_subset(sub_key, forced_flag):
        drawn_pick = jax.random.permutation(sub_key, total_size)[:pick_count].astype(jnp.int32)
        inner_pick = (jax.random.permutation(sub_key, total_size - 2)[:pick_count - 2] + 1).astype(jnp.int32)
        forced = jnp.concatenate([jnp.array([0, total_size - 1], jnp.int32), inner_pick])
        return jnp.where(forced_flag, forced, drawn_pick)
    force_flags = jnp.arange(block_count) == 0
    return jax.vmap(select_subset)(key_list, force_flags)


def coarse_map_table(key):
    map_table = subset_rows(jax.random.fold_in(key, 7), COARSE, CORNERS)
    return map_table.reshape(N_SUB, N_GRP, CORNERS)


def draw_flexibility(key, part):
    return spd_blocks(jax.random.fold_in(key, 3), ORDER).astype(jnp.bfloat16)


def draw_dirichlet_schur(key, part):
    return spd_blocks(jax.random.fold_in(key, 5), ORDER).astype(jnp.bfloat16)


def draw_coarse_map(key, part):
    return coarse_map_table(key)


def draw_coarse_rows(key, part):
    map_table = coarse_map_table(key)
    inv_key = jax.random.fold_in(jax.random.fold_in(key, 8), 0)
    factor = jax.random.normal(inv_key, (COARSE, COARSE), jnp.float32)
    product = jnp.dot(factor, factor.T, precision=lax.Precision.HIGHEST) / COARSE
    matrix = 0.5 * jnp.eye(COARSE, dtype=jnp.float32) + 0.5 * (product + product.T)
    return matrix[map_table].astype(jnp.bfloat16)


def draw_neighbors(key, part):
    half_count = NEIGHBORS // 2
    offset_span = (N_SUB - 1) // 2
    line_keys = jax.random.split(jax.random.fold_in(key, 11), N_GRP)

    def line_graph(line_key):
        perm_key, off_key = jax.random.split(line_key)
        positions = jax.random.permutation(perm_key, N_SUB).astype(jnp.int32)
        inverse = jnp.argsort(positions).astype(jnp.int32)
        offsets = (jax.random.permutation(off_key, offset_span)[:half_count] + 1).astype(jnp.int32)
        signed = jnp.concatenate([offsets, -offsets])
        neighbor_spots = (positions[:, None] + signed[None, :]) % N_SUB
        return inverse[neighbor_spots]
    line_tables = jax.vmap(line_graph)(line_keys)
    return jnp.transpose(line_tables, (1, 0, 2)).astype(jnp.int32)


def draw_interface_rows(key, part):
    picked_rows = subset_rows(jax.random.fold_in(key, 13), ORDER, NEIGHBORS * ROWS_EACH)
    return picked_rows.reshape(N_SUB, N_GRP, NEIGHBORS, ROWS_EACH)


def levels(stream_key, extent, pieces, smallest, high):
    gain, own = 1.0, jax.random.fold_in(stream_key, 6)
    for position, parts in pieces:
        heights = jnp.exp(jax.random.uniform(jax.random.fold_in(own, position), (parts,), jnp.float32, smallest / len(pieces), high / len(pieces)))
        gain = gain * jnp.repeat(heights, extent[position] // parts).reshape([-1 if axis == position else 1 for axis in range(len(extent))])
    return gain


def bell_draw(rng, extent, deviation, limit, shards=(), held_as=jnp.bfloat16):
    values = deviation * jax.random.normal(rng, extent, jnp.float32)
    if shards:
        values = values * levels(rng, extent, shards, -0.22, 0.18)
    return jnp.clip(values, -limit, limit).astype(held_as)


def setup_inputs(seed: int = 0) -> dict:
    seeds = jax.random.split(jax.random.key(seed), 9)
    return {
        "flexibility": draw_flexibility(jax.random.fold_in(seeds[8], 71), 0),
        "dirichlet_schur": draw_dirichlet_schur(jax.random.fold_in(seeds[8], 71), 0),
        "subdomain_loads": bell_draw(seeds[2], (N_SUB, N_GRP, ORDER, COLUMNS), 1.0, 6.0, ((0, 8), (1, 4))),
        "coupling": bell_draw(seeds[3], (N_SUB, N_GRP, ORDER, CORNERS), ORDER ** -0.5, 0.25, ((0, 8), (1, 4))),
        "coarse_rows": draw_coarse_rows(jax.random.fold_in(seeds[8], 71), 0),
        "neighbors": draw_neighbors(jax.random.fold_in(seeds[8], 71), 0),
        "interface_rows": draw_interface_rows(jax.random.fold_in(seeds[8], 71), 0),
        "coarse_map": draw_coarse_map(jax.random.fold_in(seeds[8], 71), 0),
    }


def apply_blocks(matrices, fields):
    block_shape = matrices.shape
    flat_matrices = matrices.reshape((-1,) + block_shape[2:])
    flat_fields = fields.reshape((-1,) + fields.shape[2:])

    def multiply(operands):
        return jnp.dot(operands[0], operands[1], preferred_element_type=jnp.float32)

    results = lax.map(multiply, (flat_matrices, flat_fields))
    return results.reshape(block_shape[:2] + results.shape[1:])


def reference(flexibility, dirichlet_schur, subdomain_loads, coupling, coarse_rows, neighbors, interface_rows, coarse_map):
    line_index = jnp.arange(N_SUB, dtype=jnp.int32)[:, None, None]
    group_index = jnp.arange(N_GRP, dtype=jnp.int32)[None, :, None]
    flat_rows = interface_rows.reshape(N_SUB, N_GRP, -1)
    pair_mask = jnp.zeros((N_SUB, N_GRP, ORDER), jnp.float32).at[line_index, group_index, flat_rows].set(1.0)
    weight = (1.0 - 0.5 * pair_mask)[..., None]
    coupling_t = jnp.swapaxes(coupling, 2, 3)
    coarse_flat = coarse_rows.reshape(-1, CORNERS, COARSE)
    corner_flat = coarse_map.reshape(-1)
    partner_lists = neighbors[neighbors, group_index]
    back_slot = jnp.argmax(partner_lists == line_index[..., None], axis=-1).astype(jnp.int32)
    their_rows = interface_rows[neighbors, group_index, back_slot]

    def jump_field(surface):
        received = surface[neighbors[..., None], group_index[..., None], their_rows]
        placed = jnp.zeros(surface.shape, jnp.float32).at[line_index[..., None], group_index[..., None], interface_rows].set(received.astype(jnp.float32))
        return surface.astype(jnp.float32) - placed

    def coarse_values(coarse_in):
        coarse_sum = jnp.zeros((COARSE, COLUMNS), jnp.float32).at[corner_flat].add(coarse_in.reshape(-1, COLUMNS)).astype(jnp.bfloat16)

        def multiply(block):
            return jnp.dot(block, coarse_sum, preferred_element_type=jnp.float32)

        return lax.map(multiply, coarse_flat).reshape(N_SUB, N_GRP, CORNERS, COLUMNS)

    def operate(direction):
        dir_half = direction.astype(jnp.bfloat16)
        local_part = apply_blocks(flexibility, dir_half)
        coarse_in = apply_blocks(coupling_t, dir_half)
        coarse_val = coarse_values(coarse_in).astype(jnp.bfloat16)
        surface = (local_part + apply_blocks(coupling, coarse_val)).astype(jnp.bfloat16)
        return jump_field(surface)

    def precondition(residual):
        scaled = (weight * residual).astype(jnp.bfloat16)
        schur_image = apply_blocks(dirichlet_schur, scaled).astype(jnp.bfloat16)
        return weight * jump_field(schur_image)

    def column_dot(first_field, second_field):
        return jnp.sum(weight * first_field * second_field, axis=(0, 1, 2))

    residual = jump_field(subdomain_loads)
    solution = jnp.zeros_like(residual)
    zfield = precondition(residual)
    direction = zfield
    inner = column_dot(residual, zfield)
    for turn_index in range(ITERATIONS):
        operated = operate(direction)
        step_size = inner / column_dot(direction, operated)
        solution = solution + step_size * direction
        residual = residual - step_size * operated
        zfield = precondition(residual)
        if turn_index + 1 < ITERATIONS:
            next_inner = column_dot(residual, zfield)
            direction = zfield + (next_inner / inner) * direction
            inner = next_inner
    return solution, zfield
```

```python
import functools

import jax
import jax.numpy as jnp
from jax import lax
from jax.experimental import pallas as pl
from jax.experimental.pallas import tpu as pltpu
from jax.sharding import PartitionSpec as P

F32 = jnp.float32
BF16 = jnp.bfloat16
VMEM_BYTES = 24 * 1024 * 1024


def round_up(value, unit):
    return -(-value // unit) * unit


class Plan:
    def __init__(self, line, groups, order, columns, corners, coarse, neighbors, each):
        self.line, self.groups = line, groups
        self.order, self.columns = order, columns
        self.corners, self.coarse = corners, coarse
        self.neighbors, self.each = neighbors, each
        self.pairs = (line - 1) * each
        self.wide = round_up(self.pairs, 128)
        self.image_at = self.pairs
        self.schur_at = 2 * self.pairs
        self.coarse_at = 3 * self.pairs
        self.tail = round_up(3 * corners + 8, 16)
        self.first = self.coarse_at + self.tail
        self.input_at = groups * corners
        self.dots_at = self.input_at + corners
        self.second = round_up(self.dots_at + 8, 16)
        self.own_at = self.pairs
        self.sums_at = self.pairs + each
        self.third = self.sums_at + 16
        self.spread = round_up(corners, 32)

    def served(self):
        return (
            self.line * self.pairs <= self.coarse
            and self.each % 16 == 0
            and self.columns == 128
            and self.wide == 128
            and self.corners % 8 == 0
            and 128 % self.spread == 0
            and (self.line * self.spread) % 128 == 0
            and self.order % 128 == 0
            and self.coarse % 128 == 0
            and self.coarse <= 128 * 256
        )

    @staticmethod
    def slot(s, t):
        return t - (1 if t > s else 0)

    @staticmethod
    def moving_slot(s, t):
        return t - jnp.where(t > s, 1, 0).astype(jnp.int32)

    def shift(self, index, step):
        if self.groups & (self.groups - 1) == 0:
            return index ^ step
        return (index + step) % self.groups

    def back(self, step):
        if self.groups & (self.groups - 1) == 0:
            return step
        return (-step) % self.groups


def dot(a, b):
    return jnp.dot(a, b, preferred_element_type=F32)


def split(value):
    high = value.astype(BF16).astype(F32)
    return high, value - high


def whole_weight(place):
    ones = jnp.ones((place.shape[1], 128), BF16)
    return 1.0 - 0.5 * dot(place, ones)


def prepare_kernel(plan, neighbors, rows, corner_map, schur, loads, coupling_t, message, place, rows_pad, map_pad):
    me = lax.axis_index("sub")
    each, pairs, wide, corners = plan.each, plan.pairs, plan.wide, plan.corners
    rows_pad[...] = jnp.full(rows_pad.shape, -1, jnp.int32)
    rows_pad[0 : plan.neighbors, 0:each] = rows[...]
    index = jnp.full((1, wide), -1, jnp.int32)
    for k in range(plan.neighbors):
        at = each * plan.moving_slot(me, neighbors[0, k])
        index = jnp.maximum(index, pltpu.roll(rows_pad[k : k + 1, :], at, 1))
    wide_index = jnp.broadcast_to(index.astype(F32), (wide, wide))
    tall_index = wide_index.T.astype(jnp.int32)
    order_rows = lax.broadcasted_iota(jnp.int32, (plan.order, wide), 0)
    place_f = jnp.where(order_rows == index, 1.0, 0.0)
    place_v = place_f.astype(BF16)
    place[...] = place_v
    lane = lax.broadcasted_iota(jnp.int32, (wide, plan.order), 1)
    pick_f = jnp.where(lane == tall_index[:, 0:1], 1.0, 0.0)
    weight_row = 1.0 - 0.5 * jnp.sum(pick_f, axis=0, keepdims=True)
    pick = pick_f.astype(BF16)
    weight = whole_weight(place_v)
    load = loads[...]
    weighted = (weight * load.astype(F32)).astype(BF16)
    image = dot(schur[...], jnp.concatenate([weighted, place_v], axis=1)).astype(BF16)
    couple = coupling_t[...]
    couple_w = (couple.astype(F32) * weight_row).astype(BF16)
    first = dot(pick, image)
    first_c = dot(couple_w, image)
    picked = dot(pick, load)
    edge = dot(couple, place_v)
    map_pad[...] = jnp.zeros(map_pad.shape, F32)
    corner_ids = corner_map[...]
    map_pad[0:1, 0:corners] = (corner_ids // 128).astype(F32)
    map_pad[1:2, 0:corners] = (corner_ids % 128).astype(F32)
    tail = [first_c[:, :128], 0.5 * first_c[:, 128:], 0.5 * edge, map_pad[...]]
    if plan.tail > 3 * corners + 8:
        tail.append(jnp.zeros((plan.tail - 3 * corners - 8, 128), F32))
    tail = jnp.concatenate(tail, axis=0).astype(BF16)
    loads_part = picked[:pairs].astype(BF16)
    image_part = first[:pairs, :128].astype(BF16)
    schur_part = (0.5 * first[:pairs, 128:]).astype(BF16)
    for d in range(plan.line):
        message[d, 0:pairs, :] = loads_part
        message[d, plan.image_at : plan.image_at + pairs, :] = image_part
        message[d, plan.schur_at : plan.schur_at + pairs, :] = schur_part
        message[d, plan.coarse_at : plan.coarse_at + plan.tail, :] = tail


def direction_kernel(plan, *refs):
    received, schur, flexibility, loads, place = refs[:5]
    coarse_refs = refs[5 : 5 + plan.groups]
    message, residual, direction, local_part, far_image = refs[5 + plan.groups : 10 + plan.groups]
    moved, images, moved_images, inputs = refs[10 + plan.groups :]
    me = lax.axis_index("sub")
    line, each, pairs, corners = plan.line, plan.each, plan.pairs, plan.corners
    zero_rows = plan.wide - pairs
    codes = []
    per_tile = 128 // plan.spread
    lane = lax.broadcasted_iota(jnp.int32, (8, 128), 1)
    for first in range(0, line, per_tile):
        code = jnp.full((1, 128), -1, jnp.int32)
        for u in range(first, first + per_tile):
            tail = received[u, plan.coarse_at : plan.coarse_at + plan.tail, :].astype(F32)
            pair_of_rows = tail[3 * corners : 3 * corners + 8]
            number = (128.0 * pair_of_rows[0:1] + pair_of_rows[1:2]).astype(jnp.int32)
            number = jnp.where(lane[0:1] < corners, number, -1)
            code = jnp.maximum(code, pltpu.roll(number, (u - first) * plan.spread, 1))
        codes.append(code)
    codes = jnp.concatenate(codes, axis=1)
    coarse_rows = lax.broadcasted_iota(jnp.int32, (plan.coarse, codes.shape[1]), 0)
    chooser = jnp.where(coarse_rows == codes, 1.0, 0.0).astype(BF16)
    coarse_all = jnp.concatenate([ref[...] for ref in coarse_refs], axis=0)
    coarse_matrix = dot(coarse_all, chooser).astype(BF16)

    tails = []
    for t in range(line):
        for d in range(line):
            if d == t:
                continue
            source, target = each * plan.slot(d, t), each * plan.slot(t, d)
            moved[t, target : target + each, :] = received[d, source : source + each, :]
        if zero_rows:
            moved[t, pairs:, :] = jnp.zeros((zero_rows, 128), BF16)
        result = dot(received[t, plan.schur_at :, :], moved[t])
        image = received[t, plan.image_at : plan.image_at + pairs, :].astype(F32) - result[:pairs]
        images[t] = image
        tails.append(result[pairs + corners : pairs + 2 * corners])
    for t in range(line):
        for d in range(line):
            if d == t:
                continue
            source, target = each * plan.slot(d, t), each * plan.slot(t, d)
            moved_images[t, target : target + each, :] = images[d, source : source + each, :]
        if zero_rows:
            moved_images[t, pairs:, :] = jnp.zeros((zero_rows, 128), F32)
        tail = received[t, plan.coarse_at :, :]
        edge = dot(tail, moved_images[t].astype(BF16))
        entry = tail.astype(F32)[:corners] - tails[t] - edge[2 * corners : 3 * corners]
        parts = [entry]
        if plan.spread > corners:
            parts.append(jnp.zeros((plan.spread - corners, 128), F32))
        inputs[t] = jnp.concatenate(parts, axis=0)
    coarse_in = inputs[...].reshape(line * plan.spread, 128).astype(BF16)
    coarse_out = dot(coarse_matrix, coarse_in)

    place_v = place[...]
    weight = whole_weight(place_v)
    right = loads[...].astype(F32) - dot(place_v, moved[me])
    image = dot(schur[...], (weight * right).astype(BF16)).astype(BF16)
    mine = moved_images[me]
    far_image[...] = mine
    field = weight * (image.astype(F32) - dot(place_v, mine.astype(BF16)))
    residual[...] = right
    direction[...] = field
    local = dot(flexibility[...], field.astype(BF16))
    local_part[...] = local
    inner_high, inner_low = split(jnp.sum(weight * right * field, axis=0, keepdims=True))
    square_high, square_low = split(jnp.sum(field * local, axis=0, keepdims=True))
    row = lax.broadcasted_iota(jnp.int32, (8, 128), 0)
    dots = jnp.zeros((8, 128), F32)
    for at, value in enumerate((inner_high, inner_low, square_high, square_low)):
        dots = jnp.where(row == at, value, dots)
    parts = [coarse_out, inputs[me][:corners], dots]
    if plan.second > plan.dots_at + 8:
        parts.append(jnp.zeros((plan.second - plan.dots_at - 8, 128), F32))
    message[...] = jnp.concatenate(parts, axis=0).astype(BF16)


def surface_kernel(plan, *refs):
    groups, corners, each, pairs = plan.groups, plan.corners, plan.each, plan.pairs
    heard = [ref[...].astype(F32) for ref in refs[:groups]]
    schur, coupling_t, place, local_part = refs[groups : groups + 4]
    message, surface = refs[groups + 4 : groups + 6]
    (image_rows,) = refs[groups + 6 :]
    me = lax.axis_index("sub")
    dots = sum(block[plan.dots_at : plan.dots_at + 8] for block in heard)
    inner = dots[0:1] + dots[1:2]
    square = dots[2:3] + dots[3:4]
    own = None
    for m in range(groups):
        value = 0.0
        for d in range(groups):
            at = corners * plan.shift(m, d)
            value = value + heard[d][at : at + corners]
        value = value.astype(BF16)
        if m == 0:
            own = value
        entry = heard[plan.back(m)][plan.input_at : plan.input_at + corners]
        square = square + jnp.sum(entry * value.astype(F32), axis=0, keepdims=True)
    lifted = lax.dot_general(
        coupling_t[...], own, (((0,), (0,)), ((), ())), preferred_element_type=F32
    )
    field = (local_part[...] + lifted).astype(BF16)
    surface[...] = field
    place_v = place[...]
    weight = whole_weight(place_v)
    scaled = (weight * field.astype(F32)).astype(BF16)
    image = dot(schur[...], scaled).astype(BF16)
    both = lax.dot_general(
        place_v,
        jnp.concatenate([field, image], axis=1),
        (((0,), (0,)), ((), ())),
        preferred_element_type=F32,
    )[:pairs]
    surface_part = both[:, :128].astype(BF16)
    image_rows[...] = both[:, 128:].reshape(plan.line - 1, each, 128)
    inner_high, inner_low = split(inner)
    square_high, square_low = split(square)
    row = lax.broadcasted_iota(jnp.int32, (16, 128), 0)
    sums = jnp.zeros((16, 128), F32)
    for at, value in enumerate((inner_high, inner_low, square_high, square_low)):
        sums = jnp.where(row == at, value, sums)
    sums = sums.astype(BF16)
    for d in range(plan.line):
        at = jnp.minimum(plan.moving_slot(me, d), plan.line - 2)
        message[d, 0:pairs, :] = surface_part
        message[d, plan.own_at : plan.own_at + each, :] = image_rows[at].astype(BF16)
        message[d, plan.sums_at :, :] = sums


def result_kernel(
    plan,
    received,
    first,
    far_image,
    residual,
    direction,
    surface,
    schur,
    place,
    solution_out,
    preconditioned,
    moved,
    far_rows,
):
    me = lax.axis_index("sub")
    line, each, pairs = plan.line, plan.each, plan.pairs
    zero_rows = plan.wide - pairs
    sums = 0.0
    for u in range(line):
        sums = sums + received[u, plan.sums_at : plan.sums_at + 16, :].astype(F32)
    step = (sums[0:1] + sums[1:2]) / (sums[2:3] + sums[3:4])
    far_rows[...] = jnp.zeros(far_rows.shape, F32)
    for t in range(line):
        for d in range(line):
            if d == t:
                continue
            source, target = each * plan.slot(d, t), each * plan.slot(t, d)
            moved[t, target : target + each, :] = received[d, source : source + each, :]
        if zero_rows:
            moved[t, pairs:, :] = jnp.zeros((zero_rows, 128), BF16)
    for t in range(line):
        at = jnp.minimum(plan.moving_slot(t, me), line - 2)
        block = first[t, pl.ds(pl.multiple_of(plan.schur_at + each * at, 16), each), :]
        change = received[t, plan.own_at : plan.own_at + each, :].astype(F32) - dot(block, moved[t])
        there = jnp.where(me == t, line - 1, plan.moving_slot(me, t))
        far_rows[there] = change
    far = far_image[...] - step * far_rows[...].reshape(line * each, 128)[: plan.wide]
    place_v = place[...]
    weight = whole_weight(place_v)
    operated = surface[...].astype(F32) - dot(place_v, moved[me])
    remaining = residual[...] - step * operated
    image = dot(schur[...], (weight * remaining).astype(BF16)).astype(BF16)
    row = lax.broadcasted_iota(jnp.int32, far.shape, 0)
    far = jnp.where(row < pairs, far, 0.0).astype(BF16)
    preconditioned[...] = weight * (image.astype(F32) - dot(place_v, far))
    solution_out[...] = step * direction[...]


def line_body(
    plan,
    flexibility,
    dirichlet_schur,
    subdomain_loads,
    coupling,
    coarse_rows,
    neighbors,
    interface_rows,
    coarse_map,
):
    line, order = plan.line, plan.order
    flex, schur, loads = flexibility[0, 0], dirichlet_schur[0, 0], subdomain_loads[0, 0]
    coupling_t = coupling[0, 0].T
    coarse = coarse_rows[0, 0]
    whole = pl.BlockSpec(memory_space=pltpu.VMEM)
    params = pltpu.CompilerParams(vmem_limit_bytes=VMEM_BYTES)

    def shape(*dims, kind=F32):
        return jax.ShapeDtypeStruct(dims, kind)

    def turn(value, step):
        pairs = [(g, plan.shift(g, step)) for g in range(plan.groups)]
        return lax.ppermute(value, "grp", pairs)

    coarse_all = [coarse]
    for step in range(1, plan.groups):
        coarse_all.append(turn(coarse, plan.back(step)))

    message, place = pl.pallas_call(
        functools.partial(prepare_kernel, plan),
        out_shape=(shape(line, plan.first, 128, kind=BF16), shape(order, plan.wide, kind=BF16)),
        in_specs=[pl.BlockSpec(memory_space=pltpu.SMEM)] + [whole] * 5,
        out_specs=(whole, whole),
        scratch_shapes=[
            pltpu.VMEM((round_up(plan.neighbors, 8), 128), jnp.int32),
            pltpu.VMEM((8, 128), F32),
        ],
        compiler_params=params,
        name="prepare",
    )(neighbors[0], interface_rows[0, 0], coarse_map[0], schur, loads, coupling_t)
    first = lax.all_to_all(message, "sub", split_axis=0, concat_axis=0, tiled=True)

    message, residual, direction, local_part, far_image = pl.pallas_call(
        functools.partial(direction_kernel, plan),
        out_shape=(
            shape(plan.second, 128, kind=BF16),
            shape(order, 128),
            shape(order, 128),
            shape(order, 128),
            shape(plan.wide, 128),
        ),
        in_specs=[whole] * (5 + plan.groups),
        out_specs=(whole,) * 5,
        scratch_shapes=[
            pltpu.VMEM((line, plan.wide, 128), BF16),
            pltpu.VMEM((line, plan.pairs, 128), F32),
            pltpu.VMEM((line, plan.wide, 128), F32),
            pltpu.VMEM((line, plan.spread, 128), F32),
        ],
        compiler_params=params,
        name="direction",
    )(first, schur, flex, loads, place, *coarse_all)
    heard = [message]
    for step in range(1, plan.groups):
        heard.append(turn(message, step))

    message, surface = pl.pallas_call(
        functools.partial(surface_kernel, plan),
        out_shape=(shape(line, plan.third, 128, kind=BF16), shape(order, 128, kind=BF16)),
        in_specs=[whole] * (plan.groups + 4),
        out_specs=(whole, whole),
        scratch_shapes=[pltpu.VMEM((line - 1, plan.each, 128), F32)],
        compiler_params=params,
        name="surface",
    )(*heard, schur, coupling_t, place, local_part)
    last = lax.all_to_all(message, "sub", split_axis=0, concat_axis=0, tiled=True)

    solved, preconditioned = pl.pallas_call(
        functools.partial(result_kernel, plan),
        out_shape=(shape(order, 128), shape(order, 128)),
        in_specs=[whole] * 8,
        out_specs=(whole, whole),
        scratch_shapes=[
            pltpu.VMEM((line, plan.wide, 128), BF16),
            pltpu.VMEM((line, plan.each, 128), F32),
        ],
        compiler_params=params,
        name="result",
    )(last, first, far_image, residual, direction, surface, schur, place)
    return solved[None, None], preconditioned[None, None]


def wide_body(
    flexibility,
    dirichlet_schur,
    subdomain_loads,
    coupling,
    coarse_rows,
    neighbors,
    interface_rows,
    coarse_map,
):
    flex_block = flexibility[0, 0]
    schur_block = dirichlet_schur[0, 0]
    loads_block = subdomain_loads[0, 0]
    couple_block = coupling[0, 0]
    coarse_block = coarse_rows[0, 0]
    neighbor_ids = neighbors[0, 0]
    row_lists = interface_rows[0, 0]
    corner_ids = coarse_map[0, 0]
    order_size = flex_block.shape[0]
    column_count = loads_block.shape[1]
    coarse_size = coarse_block.shape[1]
    line_size = lax.axis_size("sub")
    flat_rows = row_lists.reshape(-1)
    destinations = (
        jnp.arange(line_size, dtype=jnp.int32)[:, None] == neighbor_ids[None, :]
    ).astype(jnp.bfloat16)
    pair_mask = jnp.zeros((order_size,), jnp.float32).at[flat_rows].set(1.0)
    weight = (1.0 - 0.5 * pair_mask)[:, None]

    def jump_field(surface):
        picked = surface[flat_rows].reshape(row_lists.shape + (column_count,))
        outgoing = jnp.einsum(
            "dk,kjc->djc", destinations, picked, preferred_element_type=jnp.float32
        ).astype(jnp.bfloat16)
        incoming = lax.all_to_all(outgoing, "sub", split_axis=0, concat_axis=0, tiled=True)
        matched = jnp.einsum(
            "dk,djc->kjc", destinations, incoming, preferred_element_type=jnp.float32
        )
        placed = (
            jnp.zeros((order_size, column_count), jnp.float32)
            .at[flat_rows]
            .set(matched.reshape(-1, column_count))
        )
        return surface.astype(jnp.float32) - placed

    def precondition(residual):
        scaled = (weight * residual).astype(jnp.bfloat16)
        schur_image = jnp.dot(schur_block, scaled, preferred_element_type=jnp.float32).astype(
            jnp.bfloat16
        )
        return weight * jump_field(schur_image)

    def column_dot(first_field, second_field):
        return lax.psum(jnp.sum(weight * first_field * second_field, axis=0), ("sub", "grp"))

    residual = jump_field(loads_block)
    zfield = precondition(residual)
    direction = zfield
    inner = column_dot(residual, zfield)
    dir_half = direction.astype(jnp.bfloat16)
    local_part = jnp.dot(flex_block, dir_half, preferred_element_type=jnp.float32)
    coarse_in = jnp.dot(couple_block.T, dir_half, preferred_element_type=jnp.float32)
    dense_sum = jnp.zeros((coarse_size, column_count), jnp.float32).at[corner_ids].set(coarse_in)
    partial_rows = lax.psum_scatter(dense_sum, "grp", scatter_dimension=0, tiled=True)
    panel_half = lax.psum(partial_rows, "sub").astype(jnp.bfloat16)
    coarse_val = jnp.dot(
        coarse_block,
        lax.all_gather(panel_half, "grp", axis=0, tiled=True),
        preferred_element_type=jnp.float32,
    ).astype(jnp.bfloat16)
    surface = (
        local_part + jnp.dot(couple_block, coarse_val, preferred_element_type=jnp.float32)
    ).astype(jnp.bfloat16)
    operated = jump_field(surface)
    step_size = inner / column_dot(direction, operated)
    solution = step_size * direction
    residual = residual - step_size * operated
    zfield = precondition(residual)
    return (solution[None, None], zfield[None, None])


def body(*arrays):
    flexibility, _, loads, _, coarse_rows, neighbors, interface_rows, _ = arrays
    plan = Plan(
        line=lax.axis_size("sub"),
        groups=lax.axis_size("grp"),
        order=flexibility.shape[2],
        columns=loads.shape[3],
        corners=coarse_rows.shape[2],
        coarse=coarse_rows.shape[3],
        neighbors=neighbors.shape[2],
        each=interface_rows.shape[3],
    )
    if plan.served():
        return line_body(plan, *arrays)
    return wide_body(*arrays)


def solution(mesh):
    placed = (
        P("sub", "grp", None, None),
        P("sub", "grp", None, None),
        P("sub", "grp", None, None),
        P("sub", "grp", None, None),
        P("sub", "grp", None, None),
        P("sub", "grp", None),
        P("sub", "grp", None, None),
        P("sub", "grp", None),
    )
    return jax.shard_map(
        body,
        mesh=mesh,
        in_specs=placed,
        out_specs=(P("sub", "grp", None, None), P("sub", "grp", None, None)),
        check_vma=False,
    )
```

```python
import functools

import jax
import jax.numpy as jnp
from jax import lax
from jax.experimental import pallas as pl
from jax.experimental.pallas import tpu as pltpu
from jax.sharding import PartitionSpec as P

F32 = jnp.float32
BF16 = jnp.bfloat16
VMEM_BYTES = 24 * 1024 * 1024


def round_up(value, unit):
    return -(-value // unit) * unit


class Plan:
    def __init__(self, line, groups, order, columns, corners, coarse, neighbors, each):
        self.line, self.groups = line, groups
        self.order, self.columns = order, columns
        self.corners, self.coarse = corners, coarse
        self.neighbors, self.each = neighbors, each
        self.pairs = (line - 1) * each
        self.wide = round_up(self.pairs, 128)
        self.image_at = self.pairs
        self.schur_at = 2 * self.pairs
        self.coarse_at = 3 * self.pairs
        self.tail = round_up(3 * corners + 8, 16)
        self.first = self.coarse_at + self.tail
        self.input_at = groups * corners
        self.dots_at = self.input_at + corners
        self.second = round_up(self.dots_at + 8, 16)
        self.sums_at = 2 * self.pairs
        self.third = self.sums_at + 16
        self.spread = round_up(corners, 32)

    def served(self):
        return (
            self.line * self.pairs <= self.coarse
            and self.line >= 4
            and self.line & (self.line - 1) == 0
            and self.groups & (self.groups - 1) == 0
            and self.each % 16 == 0
            and self.columns == 128
            and self.wide == 128
            and self.corners % 8 == 0
            and 128 % self.spread == 0
            and (self.line * self.spread) % 128 == 0
            and self.order % 128 == 0
            and self.coarse % 128 == 0
            and self.coarse <= 128 * 256
        )

    def slot(self, a, b):
        return self.each * ((a ^ b) - 1)

    def others(self, a):
        return [b for b in range(self.line) if b != a]


def dot(a, b):
    return jnp.dot(a, b, preferred_element_type=F32)


def split(value):
    high = value.astype(BF16).astype(F32)
    return high, value - high


def whole_weight(place):
    ones = jnp.ones((place.shape[1], 128), BF16)
    return 1.0 - 0.5 * dot(place, ones)


def prepare_kernel(
    plan,
    neighbors_in,
    rows_in,
    corner_map_in,
    schur_in,
    loads_in,
    coupling_in,
    flexibility_in,
    message,
    place,
    schur,
    loads,
    coupling_t,
    flexibility,
    neighbors,
    rows,
    corner_map,
    rows_pad,
    map_pad,
    arrived,
):
    me = lax.axis_index("sub")
    each, pairs, wide, corners = plan.each, plan.pairs, plan.wide, plan.corners
    sources = (neighbors_in, rows_in, corner_map_in, loads_in, coupling_in, schur_in)
    targets = (neighbors, rows, corner_map, loads, coupling_t, schur)
    sources += (flexibility_in,)
    targets += (flexibility,)
    copies = [
        pltpu.make_async_copy(source, target, arrived.at[at])
        for at, (source, target) in enumerate(zip(sources, targets))
    ]
    for copy in copies:
        copy.start()
    rows_pad[...] = jnp.zeros(rows_pad.shape, jnp.int32)
    map_pad[...] = jnp.zeros(map_pad.shape, F32)
    copies[0].wait()
    copies[1].wait()
    for k in range(plan.neighbors):
        rows_pad[k : k + 1, 0:each] = rows[k]
    spread = rows_pad[...]
    reach = each
    while reach < wide:
        spread = spread + pltpu.roll(spread, reach, 1)
        reach *= 2
    lane = lax.broadcasted_iota(jnp.int32, (1, wide), 1)
    slots = neighbors[...] ^ me
    index = jnp.full((1, wide), -1, jnp.int32)
    for k in range(plan.neighbors):
        index = jnp.where(lane // each + 1 == slots[0:1, k : k + 1], spread[k : k + 1], index)
    wide_index = jnp.broadcast_to(index.astype(F32), (wide, wide))
    tall_index = wide_index.T.astype(jnp.int32)
    order_rows = lax.broadcasted_iota(jnp.int32, (plan.order, wide), 0)
    place_v = jnp.where(order_rows == index, 1.0, 0.0).astype(BF16)
    place[...] = place_v
    order_lanes = lax.broadcasted_iota(jnp.int32, (wide, plan.order), 1)
    pick_f = jnp.where(order_lanes == tall_index[:, 0:1], 1.0, 0.0)
    weight_row = 1.0 - 0.5 * jnp.sum(pick_f, axis=0, keepdims=True)
    pick = pick_f.astype(BF16)
    weight = whole_weight(place_v)
    copies[2].wait()
    corner_ids = corner_map[...]
    map_pad[0:1, 0:corners] = (corner_ids // 128).astype(F32)
    map_pad[1:2, 0:corners] = (corner_ids % 128).astype(F32)
    copies[3].wait()
    load = loads[...]
    weighted = (weight * load.astype(F32)).astype(BF16)
    message[0:pairs, :] = dot(pick, load)[:pairs].astype(BF16)
    copies[4].wait()
    couple = coupling_t[...]
    couple_w = (couple.astype(F32) * weight_row).astype(BF16)
    edge = dot(couple, place_v)
    copies[5].wait()
    image = dot(schur[...], jnp.concatenate([weighted, place_v], axis=1)).astype(BF16)
    first = dot(pick, image)
    first_c = dot(couple_w, image)
    tail = [first_c[:, :128], 0.5 * first_c[:, 128:], 0.5 * edge, map_pad[...]]
    if plan.tail > 3 * corners + 8:
        tail.append(jnp.zeros((plan.tail - 3 * corners - 8, 128), F32))
    message[plan.image_at : plan.image_at + pairs, :] = first[:pairs, :128].astype(BF16)
    message[plan.schur_at : plan.schur_at + pairs, :] = (0.5 * first[:pairs, 128:]).astype(BF16)
    message[plan.coarse_at :, :] = jnp.concatenate(tail, axis=0).astype(BF16)
    copies[6].wait()


def direction_kernel(plan, *refs):
    line, each, pairs, corners = plan.line, plan.each, plan.pairs, plan.corners
    received, refs = refs[:line], refs[line:]
    coarse_refs, refs = refs[: plan.groups], refs[plan.groups :]
    schur, flexibility, loads, place = refs[:4]
    message, residual, direction, local_part, far_image = refs[4:9]
    moved, images, moved_images, inputs = refs[9:]
    zero_rows = plan.wide - pairs
    codes = []
    per_tile = 128 // plan.spread
    lane = lax.broadcasted_iota(jnp.int32, (8, 128), 1)
    for first in range(0, line, per_tile):
        code = jnp.full((1, 128), -1, jnp.int32)
        for u in range(first, first + per_tile):
            tail = received[u][plan.coarse_at :, :].astype(F32)
            pair_of_rows = tail[3 * corners : 3 * corners + 8]
            number = (128.0 * pair_of_rows[0:1] + pair_of_rows[1:2]).astype(jnp.int32)
            number = jnp.where(lane[0:1] < corners, number, -1)
            code = jnp.maximum(code, pltpu.roll(number, (u - first) * plan.spread, 1))
        codes.append(code)
    codes = jnp.concatenate(codes, axis=1)
    coarse_rows = lax.broadcasted_iota(jnp.int32, (plan.coarse, codes.shape[1]), 0)
    chooser = jnp.where(coarse_rows == codes, 1.0, 0.0).astype(BF16)
    coarse_all = jnp.concatenate([ref[...] for ref in coarse_refs], axis=0)
    coarse_matrix = dot(coarse_all, chooser).astype(BF16)

    tails = []
    for t in range(line):
        for d in plan.others(t):
            at = plan.slot(t, d)
            moved[t, at : at + each, :] = received[d][at : at + each, :]
        if zero_rows:
            moved[t, pairs:, :] = jnp.zeros((zero_rows, 128), BF16)
        result = dot(received[t][plan.schur_at :, :], moved[t])
        image = received[t][plan.image_at : plan.image_at + pairs, :].astype(F32) - result[:pairs]
        images[t] = image
        tails.append(result[pairs + corners : pairs + 2 * corners])
    for t in range(line):
        for d in plan.others(t):
            at = plan.slot(t, d)
            moved_images[t, at : at + each, :] = images[d, at : at + each, :]
        if zero_rows:
            moved_images[t, pairs:, :] = jnp.zeros((zero_rows, 128), F32)
        tail = received[t][plan.coarse_at :, :]
        edge = dot(tail, moved_images[t].astype(BF16))
        entry = tail.astype(F32)[:corners] - tails[t] - edge[2 * corners : 3 * corners]
        parts = [entry]
        if plan.spread > corners:
            parts.append(jnp.zeros((plan.spread - corners, 128), F32))
        inputs[t] = jnp.concatenate(parts, axis=0)
    coarse_in = inputs[...].reshape(line * plan.spread, 128).astype(BF16)
    coarse_out = dot(coarse_matrix, coarse_in)

    place_v = place[...]
    weight = whole_weight(place_v)
    right = loads[...].astype(F32) - dot(place_v, moved[0])
    image = dot(schur[...], (weight * right).astype(BF16)).astype(BF16)
    mine = moved_images[0]
    far_image[...] = mine
    field = weight * (image.astype(F32) - dot(place_v, mine.astype(BF16)))
    residual[...] = right
    direction[...] = field
    local = dot(flexibility[...], field.astype(BF16))
    local_part[...] = local
    inner_high, inner_low = split(jnp.sum(weight * right * field, axis=0, keepdims=True))
    square_high, square_low = split(jnp.sum(field * local, axis=0, keepdims=True))
    row = lax.broadcasted_iota(jnp.int32, (8, 128), 0)
    dots = jnp.zeros((8, 128), F32)
    for at, value in enumerate((inner_high, inner_low, square_high, square_low)):
        dots = jnp.where(row == at, value, dots)
    parts = [coarse_out, inputs[0][:corners], dots]
    if plan.second > plan.dots_at + 8:
        parts.append(jnp.zeros((plan.second - plan.dots_at - 8, 128), F32))
    message[...] = jnp.concatenate(parts, axis=0).astype(BF16)


def surface_kernel(plan, *refs):
    groups, corners, pairs = plan.groups, plan.corners, plan.pairs
    heard = [ref[...].astype(F32) for ref in refs[:groups]]
    schur, coupling_t, place, local_part = refs[groups : groups + 4]
    message, surface = refs[groups + 4 :]
    dots = sum(block[plan.dots_at : plan.dots_at + 8] for block in heard)
    inner = dots[0:1] + dots[1:2]
    square = dots[2:3] + dots[3:4]
    own = None
    for m in range(groups):
        value = 0.0
        for d in range(groups):
            at = corners * (m ^ d)
            value = value + heard[d][at : at + corners]
        value = value.astype(BF16)
        if m == 0:
            own = value
        entry = heard[m][plan.input_at : plan.input_at + corners]
        square = square + jnp.sum(entry * value.astype(F32), axis=0, keepdims=True)
    lifted = lax.dot_general(
        coupling_t[...], own, (((0,), (0,)), ((), ())), preferred_element_type=F32
    )
    field = (local_part[...] + lifted).astype(BF16)
    surface[...] = field
    place_v = place[...]
    weight = whole_weight(place_v)
    scaled = (weight * field.astype(F32)).astype(BF16)
    image = dot(schur[...], scaled).astype(BF16)
    both = lax.dot_general(
        place_v,
        jnp.concatenate([field, image], axis=1),
        (((0,), (0,)), ((), ())),
        preferred_element_type=F32,
    )[:pairs]
    message[0:pairs, :] = both[:, :128].astype(BF16)
    message[pairs : 2 * pairs, :] = both[:, 128:].astype(BF16)
    inner_high, inner_low = split(inner)
    square_high, square_low = split(square)
    row = lax.broadcasted_iota(jnp.int32, (16, 128), 0)
    sums = jnp.zeros((16, 128), F32)
    for at, value in enumerate((inner_high, inner_low, square_high, square_low)):
        sums = jnp.where(row == at, value, sums)
    message[plan.sums_at :, :] = sums.astype(BF16)


def result_kernel(plan, *refs):
    line, each, pairs = plan.line, plan.each, plan.pairs
    received, first, refs = refs[:line], refs[line : 2 * line - 1], refs[2 * line - 1 :]
    far_image, residual, direction, surface, schur, place = refs[:6]
    solution_out, preconditioned, moved, far_rows = refs[6:]
    zero_rows = plan.wide - pairs
    sums = 0.0
    for block in received:
        sums = sums + block[plan.sums_at :, :].astype(F32)
    step = (sums[0:1] + sums[1:2]) / (sums[2:3] + sums[3:4])
    for t in range(line):
        for d in plan.others(t):
            at = plan.slot(t, d)
            moved[t, at : at + each, :] = received[d][at : at + each, :]
        if zero_rows:
            moved[t, pairs:, :] = jnp.zeros((zero_rows, 128), BF16)
    if zero_rows:
        far_rows[pairs:, :] = jnp.zeros((zero_rows, 128), F32)
    for t in range(1, line):
        at = plan.slot(0, t)
        block = first[t - 1][plan.schur_at + at : plan.schur_at + at + each, :]
        image = received[t][pairs + at : pairs + at + each, :].astype(F32)
        far_rows[at : at + each, :] = image - dot(block, moved[t])
    far = far_image[...] - step * far_rows[...]
    place_v = place[...]
    weight = whole_weight(place_v)
    operated = surface[...].astype(F32) - dot(place_v, moved[0])
    remaining = residual[...] - step * operated
    image = dot(schur[...], (weight * remaining).astype(BF16)).astype(BF16)
    preconditioned[...] = weight * (image.astype(F32) - dot(place_v, far.astype(BF16)))
    solution_out[...] = step * direction[...]


def line_body(
    plan,
    flexibility,
    dirichlet_schur,
    subdomain_loads,
    coupling,
    coarse_rows,
    neighbors,
    interface_rows,
    coarse_map,
):
    line, order = plan.line, plan.order
    flex, schur, loads = flexibility[0, 0], dirichlet_schur[0, 0], subdomain_loads[0, 0]
    coupling_t = coupling[0, 0].T
    coarse = coarse_rows[0, 0]
    rows = jnp.transpose(interface_rows, (0, 2, 1, 3))[0]
    whole = pl.BlockSpec(memory_space=pltpu.VMEM)
    outside = pl.BlockSpec(memory_space=pltpu.HBM)
    params = pltpu.CompilerParams(vmem_limit_bytes=VMEM_BYTES)

    def shape(*dims, kind=F32):
        return jax.ShapeDtypeStruct(dims, kind)

    def swap(value, axis, distance):
        size = lax.axis_size(axis)
        return lax.ppermute(value, axis, [(at, at ^ distance) for at in range(size)])

    def line_blocks(value, riders=()):
        blocks = [value] + [None] * (line - 1)
        moved = []
        for far in reversed(range(2, line, 2)):
            blocks[far] = swap(value, "sub", far)
        blocks[1] = swap(value, "sub", 1)
        for far in reversed(range(2, line, 2)):
            block = blocks[far]
            if len(moved) < len(riders):
                rider, distance = riders[len(moved)]
                block, rider = lax.optimization_barrier((block, rider))
                moved.append(swap(rider, "grp", distance))
                blocks[far] = block
            blocks[far + 1] = swap(block, "sub", 1)
        for rider, distance in riders[len(moved) :]:
            moved.append(swap(rider, "grp", distance))
        return blocks, moved

    lists = (neighbors[0], rows, coarse_map[0])
    kept = (schur, loads, coupling_t, flex)
    kept = tuple(pltpu.with_memory_space_constraint(array, pltpu.HBM) for array in kept)
    message, place, schur, loads, coupling_t, flex = pl.pallas_call(
        functools.partial(prepare_kernel, plan),
        out_shape=(shape(plan.first, 128, kind=BF16), shape(order, plan.wide, kind=BF16))
        + tuple(shape(*array.shape, kind=BF16) for array in kept),
        in_specs=[outside] * 7,
        out_specs=(whole,) * 6,
        scratch_shapes=[pltpu.VMEM(array.shape, array.dtype) for array in lists]
        + [
            pltpu.VMEM((round_up(plan.neighbors, 8), plan.wide), jnp.int32),
            pltpu.VMEM((8, 128), F32),
            pltpu.SemaphoreType.DMA((7,)),
        ],
        compiler_params=params,
        name="prepare",
    )(*lists, *kept)
    riders = [(coarse, distance) for distance in reversed(range(1, plan.groups))]
    first, moved = line_blocks(message, riders)
    coarse_all = [coarse] + moved[::-1]

    message, residual, direction, local_part, far_image = pl.pallas_call(
        functools.partial(direction_kernel, plan),
        out_shape=(
            shape(plan.second, 128, kind=BF16),
            shape(order, 128),
            shape(order, 128),
            shape(order, 128),
            shape(plan.wide, 128),
        ),
        in_specs=[whole] * (line + plan.groups + 4),
        out_specs=(whole,) * 5,
        scratch_shapes=[
            pltpu.VMEM((line, plan.wide, 128), BF16),
            pltpu.VMEM((line, plan.pairs, 128), F32),
            pltpu.VMEM((line, plan.wide, 128), F32),
            pltpu.VMEM((line, plan.spread, 128), F32),
        ],
        compiler_params=params,
        name="direction",
    )(*first, *coarse_all, schur, flex, loads, place)
    heard = [message]
    for step in range(1, plan.groups):
        heard.append(swap(message, "grp", step))

    message, surface = pl.pallas_call(
        functools.partial(surface_kernel, plan),
        out_shape=(shape(plan.third, 128, kind=BF16), shape(order, 128, kind=BF16)),
        in_specs=[whole] * (plan.groups + 4),
        out_specs=(whole, whole),
        compiler_params=params,
        name="surface",
    )(*heard, schur, coupling_t, place, local_part)
    last, _ = line_blocks(message)

    solved, preconditioned = pl.pallas_call(
        functools.partial(result_kernel, plan),
        out_shape=(shape(order, 128), shape(order, 128)),
        in_specs=[whole] * (2 * line + 5),
        out_specs=(whole, whole),
        scratch_shapes=[
            pltpu.VMEM((line, plan.wide, 128), BF16),
            pltpu.VMEM((plan.wide, 128), F32),
        ],
        compiler_params=params,
        name="result",
    )(*last, *first[1:], far_image, residual, direction, surface, schur, place)
    return solved[None, None], preconditioned[None, None]


def wide_body(
    flexibility,
    dirichlet_schur,
    subdomain_loads,
    coupling,
    coarse_rows,
    neighbors,
    interface_rows,
    coarse_map,
):
    flex_block = flexibility[0, 0]
    schur_block = dirichlet_schur[0, 0]
    loads_block = subdomain_loads[0, 0]
    couple_block = coupling[0, 0]
    coarse_block = coarse_rows[0, 0]
    neighbor_ids = neighbors[0, 0]
    row_lists = interface_rows[0, 0]
    corner_ids = coarse_map[0, 0]
    order_size = flex_block.shape[0]
    column_count = loads_block.shape[1]
    coarse_size = coarse_block.shape[1]
    line_size = lax.axis_size("sub")
    flat_rows = row_lists.reshape(-1)
    destinations = (
        jnp.arange(line_size, dtype=jnp.int32)[:, None] == neighbor_ids[None, :]
    ).astype(jnp.bfloat16)
    pair_mask = jnp.zeros((order_size,), jnp.float32).at[flat_rows].set(1.0)
    weight = (1.0 - 0.5 * pair_mask)[:, None]

    def jump_field(surface):
        picked = surface[flat_rows].reshape(row_lists.shape + (column_count,))
        outgoing = jnp.einsum(
            "dk,kjc->djc", destinations, picked, preferred_element_type=jnp.float32
        ).astype(jnp.bfloat16)
        incoming = lax.all_to_all(outgoing, "sub", split_axis=0, concat_axis=0, tiled=True)
        matched = jnp.einsum(
            "dk,djc->kjc", destinations, incoming, preferred_element_type=jnp.float32
        )
        placed = (
            jnp.zeros((order_size, column_count), jnp.float32)
            .at[flat_rows]
            .set(matched.reshape(-1, column_count))
        )
        return surface.astype(jnp.float32) - placed

    def precondition(residual):
        scaled = (weight * residual).astype(jnp.bfloat16)
        schur_image = jnp.dot(schur_block, scaled, preferred_element_type=jnp.float32).astype(
            jnp.bfloat16
        )
        return weight * jump_field(schur_image)

    def column_dot(first_field, second_field):
        return lax.psum(jnp.sum(weight * first_field * second_field, axis=0), ("sub", "grp"))

    residual = jump_field(loads_block)
    zfield = precondition(residual)
    direction = zfield
    inner = column_dot(residual, zfield)
    dir_half = direction.astype(jnp.bfloat16)
    local_part = jnp.dot(flex_block, dir_half, preferred_element_type=jnp.float32)
    coarse_in = jnp.dot(couple_block.T, dir_half, preferred_element_type=jnp.float32)
    dense_sum = jnp.zeros((coarse_size, column_count), jnp.float32).at[corner_ids].set(coarse_in)
    partial_rows = lax.psum_scatter(dense_sum, "grp", scatter_dimension=0, tiled=True)
    panel_half = lax.psum(partial_rows, "sub").astype(jnp.bfloat16)
    coarse_val = jnp.dot(
        coarse_block,
        lax.all_gather(panel_half, "grp", axis=0, tiled=True),
        preferred_element_type=jnp.float32,
    ).astype(jnp.bfloat16)
    surface = (
        local_part + jnp.dot(couple_block, coarse_val, preferred_element_type=jnp.float32)
    ).astype(jnp.bfloat16)
    operated = jump_field(surface)
    step_size = inner / column_dot(direction, operated)
    solution = step_size * direction
    residual = residual - step_size * operated
    zfield = precondition(residual)
    return (solution[None, None], zfield[None, None])


def body(*arrays):
    flexibility, _, loads, _, coarse_rows, neighbors, interface_rows, _ = arrays
    plan = Plan(
        line=lax.axis_size("sub"),
        groups=lax.axis_size("grp"),
        order=flexibility.shape[2],
        columns=loads.shape[3],
        corners=coarse_rows.shape[2],
        coarse=coarse_rows.shape[3],
        neighbors=neighbors.shape[2],
        each=interface_rows.shape[3],
    )
    if plan.served():
        return line_body(plan, *arrays)
    return wide_body(*arrays)


def solution(mesh):
    placed = (
        P("sub", "grp", None, None),
        P("sub", "grp", None, None),
        P("sub", "grp", None, None),
        P("sub", "grp", None, None),
        P("sub", "grp", None, None),
        P("sub", "grp", None),
        P("sub", "grp", None, None),
        P("sub", "grp", None),
    )
    return jax.shard_map(
        body,
        mesh=mesh,
        in_specs=placed,
        out_specs=(P("sub", "grp", None, None), P("sub", "grp", None, None)),
        check_vma=False,
    )
```

```python
import functools

import jax
import jax.numpy as jnp
from jax import lax
from jax.experimental import pallas as pl
from jax.experimental.pallas import tpu as pltpu
from jax.sharding import PartitionSpec as P

F32 = jnp.float32
BF16 = jnp.bfloat16
VMEM_BYTES = 24 * 1024 * 1024


def round_up(value, unit):
    return -(-value // unit) * unit


class Plan:
    def __init__(self, line, groups, order, columns, corners, coarse, neighbors, each):
        self.line, self.groups = line, groups
        self.order, self.columns = order, columns
        self.corners, self.coarse = corners, coarse
        self.neighbors, self.each = neighbors, each
        self.last = line - 1
        self.pairs = neighbors * each
        self.wide = round_up(self.pairs, 128)
        self.image_at = self.pairs
        self.schur_at = 2 * self.pairs
        self.coarse_at = 3 * self.pairs
        self.tail = round_up(2 * corners, 16)
        self.first = self.coarse_at + self.tail
        self.input_at = groups * corners
        self.dots_at = self.input_at + corners
        self.second = round_up(self.dots_at + 8, 16)
        self.sums_at = self.pairs + 2 * each
        self.third = self.sums_at + 16
        self.spread = round_up(corners, 32)

    def served(self):
        return (
            self.line >= 4
            and self.line & (self.line - 1) == 0
            and self.groups & (self.groups - 1) == 0
            and self.neighbors == self.line - 2
            and self.each % 16 == 0
            and self.columns == 128
            and self.wide == 128
            and self.pairs + self.corners <= 128
            and self.corners % 8 == 0
            and self.corners >= 8
            and 128 % self.spread == 0
            and (self.line * self.spread) % 128 == 0
            and self.order % 128 == 0
            and self.coarse % 128 == 0
            and self.coarse <= 128 * 256
        )

    def slots(self):
        return range(self.neighbors)

    def rows(self, slot):
        return slice(self.each * slot, self.each * (slot + 1))


def dot(a, b):
    return jnp.dot(a, b, preferred_element_type=F32)


def dot_over_rows(a, b):
    return lax.dot_general(a, b, (((0,), (0,)), ((), ())), preferred_element_type=F32)


def dot_over_lanes(a, b):
    return lax.dot_general(a, b, (((1,), (1,)), ((), ())), preferred_element_type=F32)


def split(value):
    high = value.astype(BF16).astype(F32)
    return high, value - high


def stack_rows(values, height):
    row = lax.broadcasted_iota(jnp.int32, (height, 128), 0)
    stacked = jnp.zeros((height, 128), F32)
    for at, value in enumerate(values):
        stacked = jnp.where(row == at, value, stacked)
    return stacked


def whole_weight(place):
    ones = jnp.ones((place.shape[1], 128), BF16)
    return 1.0 - 0.5 * dot(place, ones)


def missing_of(plan, tail):
    at = plan.corners + 2
    return jnp.broadcast_to(tail[at : at + 1, plan.pairs : plan.pairs + 1], (plan.each, 128))


def last_block(plan, missing, blocks):
    found = jnp.zeros((plan.each, 128), F32)
    for slot in plan.slots():
        found = jnp.where(missing == slot + 1.0, blocks(slot), found)
    return found


def gather_pairs(plan, t, missing, blocks, store):
    far = t ^ plan.last
    last = last_block(plan, missing[far], functools.partial(blocks, far))
    for slot in plan.slots():
        value = blocks(t ^ (slot + 1), slot)
        store(slot, jnp.where(missing[t] == slot + 1.0, last, value))


def prepare_kernel(
    plan,
    neighbors_in,
    rows_in,
    corner_map_in,
    schur_in,
    loads_in,
    coupling_in,
    flexibility_in,
    message,
    place,
    schur,
    loads,
    coupling_t,
    flexibility,
    neighbors,
    rows,
    corner_map,
    rows_pad,
    map_pad,
    couple_pad,
    arrived,
):
    me = lax.axis_index("sub")
    each, pairs, wide, corners = plan.each, plan.pairs, plan.wide, plan.corners
    sources = (neighbors_in, rows_in, corner_map_in, loads_in, coupling_in, schur_in)
    targets = (neighbors, rows, corner_map, loads, coupling_t, schur)
    sources += (flexibility_in,)
    targets += (flexibility,)
    copies = [
        pltpu.make_async_copy(source, target, arrived.at[at])
        for at, (source, target) in enumerate(zip(sources, targets))
    ]
    for copy in copies:
        copy.start()
    rows_pad[...] = jnp.zeros(rows_pad.shape, jnp.int32)
    map_pad[...] = jnp.zeros(map_pad.shape, F32)
    couple_pad[...] = jnp.zeros(couple_pad.shape, BF16)
    copies[0].wait()
    copies[1].wait()
    for k in range(plan.neighbors):
        rows_pad[k : k + 1, 0:each] = rows[k]
    spread = rows_pad[...]
    reach = each
    while reach < wide:
        spread = spread + pltpu.roll(spread, reach, 1)
        reach *= 2
    lane = lax.broadcasted_iota(jnp.int32, (1, wide), 1)
    distances = neighbors[...] ^ me
    missing = jnp.full((1, 1), plan.line * (plan.line - 1) // 2, jnp.int32)
    for k in range(plan.neighbors):
        missing = missing - distances[0:1, k : k + 1]
    index = jnp.full((1, wide), -1, jnp.int32)
    for k in range(plan.neighbors):
        distance = distances[0:1, k : k + 1]
        home = jnp.where(distance == plan.last, missing, distance)
        index = jnp.where(lane // each + 1 == home, spread[k : k + 1], index)
    wide_index = jnp.broadcast_to(index.astype(F32), (wide, wide))
    tall_index = wide_index.T.astype(jnp.int32)
    order_rows = lax.broadcasted_iota(jnp.int32, (plan.order, wide), 0)
    place_v = jnp.where(order_rows == index, 1.0, 0.0).astype(BF16)
    place[...] = place_v
    order_lanes = lax.broadcasted_iota(jnp.int32, (wide, plan.order), 1)
    pick_f = jnp.where(order_lanes == tall_index[:, 0:1], 1.0, 0.0)
    weight_row = 1.0 - 0.5 * jnp.sum(pick_f, axis=0, keepdims=True)
    pick = pick_f.astype(BF16)[:pairs]
    weight = whole_weight(place_v)
    copies[2].wait()
    corner_ids = corner_map[...]
    map_pad[0:1, 0:corners] = (corner_ids // 128).astype(F32)
    map_pad[1:2, 0:corners] = (corner_ids % 128).astype(F32)
    map_pad[2:3, :] = jnp.broadcast_to(missing.astype(F32), (1, 128))
    extra_lane = lax.broadcasted_iota(jnp.int32, (8, 128), 1)
    extra = jnp.where(extra_lane >= pairs, pltpu.roll(map_pad[...], pairs, 1), 0.0)
    copies[3].wait()
    load = loads[...]
    weighted = (weight * load.astype(F32)).astype(BF16)
    message[0:pairs, :] = dot(pick, load).astype(BF16)
    copies[4].wait()
    couple = coupling_t[...]
    couple_w = (couple.astype(F32) * weight_row).astype(BF16)
    room = round_up(corners, 16)
    padded = couple
    if room > corners:
        zeros = jnp.zeros((room - corners, plan.order), F32)
        padded = jnp.concatenate([couple.astype(F32), zeros], axis=0).astype(BF16)
    couple_pad[pairs : pairs + room, :] = padded
    edge = dot_over_lanes(pick, couple_pad[...])
    copies[5].wait()
    image = dot(schur[...], jnp.concatenate([weighted, place_v], axis=1)).astype(BF16)
    first = dot(pick, image)
    first_c = dot(couple_w, image)
    pair_part = 0.5 * first_c[:, 128:]
    tail = [first_c[:, :128], pair_part[:8] + extra]
    if corners > 8:
        tail.append(pair_part[8:])
    if plan.tail > 2 * corners:
        tail.append(jnp.zeros((plan.tail - 2 * corners, 128), F32))
    message[plan.image_at : plan.image_at + pairs, :] = first[:, :128].astype(BF16)
    message[plan.schur_at : plan.coarse_at, :] = (0.5 * (first[:, 128:] + edge)).astype(BF16)
    message[plan.coarse_at :, :] = jnp.concatenate(tail, axis=0).astype(BF16)
    copies[6].wait()


def direction_kernel(plan, *refs):
    line, pairs, corners = plan.line, plan.pairs, plan.corners
    received, refs = refs[:line], refs[line:]
    coarse_refs, refs = refs[: plan.groups], refs[plan.groups :]
    schur, flexibility, loads, place = refs[:4]
    message, residual, direction, local_part, far_image = refs[4:9]
    moved, images, moved_images, inputs = refs[9:]
    tails = [block[plan.coarse_at :, :].astype(F32) for block in received]
    missing = [missing_of(plan, tail) for tail in tails]
    codes = []
    per_tile = 128 // plan.spread
    lane = lax.broadcasted_iota(jnp.int32, (1, 128), 1)
    for first in range(0, line, per_tile):
        code = jnp.full((1, 128), -1, jnp.int32)
        for u in range(first, first + per_tile):
            number = pltpu.roll(tails[u][corners : corners + 8], 128 - pairs, 1)
            number = (128.0 * number[0:1] + number[1:2]).astype(jnp.int32)
            number = jnp.where(lane < corners, number, -1)
            code = jnp.maximum(code, pltpu.roll(number, (u - first) * plan.spread, 1))
        codes.append(code)
    codes = jnp.concatenate(codes, axis=1)
    coarse_rows = lax.broadcasted_iota(jnp.int32, (plan.coarse, codes.shape[1]), 0)
    chooser = jnp.where(coarse_rows == codes, 1.0, 0.0).astype(BF16)
    coarse_all = jnp.concatenate([ref[...] for ref in coarse_refs], axis=0)
    coarse_matrix = dot(coarse_all, chooser).astype(BF16)

    def loads_block(d, slot):
        return received[d][plan.rows(slot), :].astype(F32)

    def image_block(d, slot):
        return images[d, plan.rows(slot), :]

    changes = []
    for t in range(line):

        def store_loads(slot, value, t=t):
            moved[t, plan.rows(slot), :] = value.astype(BF16)

        gather_pairs(plan, t, missing, loads_block, store_loads)
        if plan.wide > pairs:
            moved[t, pairs:, :] = jnp.zeros((plan.wide - pairs, 128), BF16)
        result = dot(received[t][plan.schur_at :, :], moved[t])
        image = received[t][plan.image_at : plan.schur_at, :].astype(F32)
        images[t] = image - result[:pairs]
        changes.append(result[pairs + corners : pairs + 2 * corners])
    for t in range(line):

        def store_image(slot, value, t=t):
            moved_images[t, plan.rows(slot), :] = value

        gather_pairs(plan, t, missing, image_block, store_image)
        coupled = received[t][plan.schur_at : plan.coarse_at, :]
        edge = dot_over_rows(coupled, moved_images[t].astype(BF16))
        entry = tails[t][:corners] - changes[t] - edge[pairs : pairs + corners]
        parts = [entry]
        if plan.spread > corners:
            parts.append(jnp.zeros((plan.spread - corners, 128), F32))
        inputs[t] = jnp.concatenate(parts, axis=0)
    coarse_in = inputs[...].reshape(line * plan.spread, 128).astype(BF16)
    coarse_out = dot(coarse_matrix, coarse_in)

    place_v = place[...]
    weight = whole_weight(place_v)
    right = loads[...].astype(F32) - dot(place_v, moved[0])
    image = dot(schur[...], (weight * right).astype(BF16)).astype(BF16)
    mine = moved_images[0]
    if plan.wide > pairs:
        mine = jnp.concatenate([mine, jnp.zeros((plan.wide - pairs, 128), F32)], axis=0)
    far_image[...] = mine
    field = weight * (image.astype(F32) - dot(place_v, mine.astype(BF16)))
    residual[...] = right
    direction[...] = field
    local = dot(flexibility[...], field.astype(BF16))
    local_part[...] = local
    inner = split(jnp.sum(weight * right * field, axis=0, keepdims=True))
    square = split(jnp.sum(field * local, axis=0, keepdims=True))
    parts = [coarse_out, inputs[0][:corners], stack_rows(inner + square, 8)]
    if plan.second > plan.dots_at + 8:
        parts.append(jnp.zeros((plan.second - plan.dots_at - 8, 128), F32))
    message[...] = jnp.concatenate(parts, axis=0).astype(BF16)


def surface_kernel(plan, *refs):
    groups, corners, pairs = plan.groups, plan.corners, plan.pairs
    heard = [ref[...].astype(F32) for ref in refs[:groups]]
    own_first, schur, coupling_t, place, local_part = refs[groups : groups + 5]
    surface, messages = refs[groups + 5], refs[groups + 6 :]
    dots = sum(block[plan.dots_at : plan.dots_at + 8] for block in heard)
    inner = dots[0:1] + dots[1:2]
    square = dots[2:3] + dots[3:4]
    own = None
    for m in range(groups):
        value = 0.0
        for d in range(groups):
            at = corners * (m ^ d)
            value = value + heard[d][at : at + corners]
        value = value.astype(BF16)
        if m == 0:
            own = value
        entry = heard[m][plan.input_at : plan.input_at + corners]
        square = square + jnp.sum(entry * value.astype(F32), axis=0, keepdims=True)
    field = (local_part[...] + dot_over_rows(coupling_t[...], own)).astype(BF16)
    surface[...] = field
    place_v = place[...]
    weight = whole_weight(place_v)
    scaled = (weight * field.astype(F32)).astype(BF16)
    image = dot(schur[...], scaled).astype(BF16)
    both = dot_over_rows(place_v, jnp.concatenate([field, image], axis=1))[:pairs]
    surface_part = both[:, :128].astype(BF16)
    sums = stack_rows(split(inner) + split(square), 16).astype(BF16)
    missing = missing_of(plan, own_first[plan.coarse_at :, :].astype(F32))

    def image_part(distance):
        if distance == 0:
            return jnp.zeros((plan.each, 128), F32)
        if distance == plan.last:
            return last_block(plan, missing, lambda slot: image_part(slot + 1))
        return both[plan.rows(distance - 1), 128:]

    for far, message in zip(range(0, plan.line, 2), messages):
        message[0:pairs, :] = surface_part
        message[pairs : pairs + plan.each, :] = image_part(far).astype(BF16)
        message[pairs + plan.each : plan.sums_at, :] = image_part(far + 1).astype(BF16)
        message[plan.sums_at :, :] = sums


def result_kernel(plan, *refs):
    line, pairs, each = plan.line, plan.pairs, plan.each
    received, first, refs = refs[:line], refs[line : 2 * line], refs[2 * line :]
    far_image, residual, direction, surface, schur, place = refs[:6]
    solution_out, preconditioned_out = refs[6:8]
    moved, far_rows, solved, preconditioned, sent = refs[8:]
    sums = 0.0
    for block in received:
        sums = sums + block[plan.sums_at :, :].astype(F32)
    step = (sums[0:1] + sums[1:2]) / (sums[2:3] + sums[3:4])
    solved[...] = step * direction[...]
    solution_copy = pltpu.make_async_copy(solved, solution_out, sent.at[0])
    solution_copy.start()
    missing = [missing_of(plan, block[plan.coarse_at :, :].astype(F32)) for block in first]

    def surface_block(d, slot):
        return received[d][plan.rows(slot), :].astype(F32)

    changes = []
    for t in range(line):

        def store_surface(slot, value, t=t):
            moved[t, plan.rows(slot), :] = value.astype(BF16)

        gather_pairs(plan, t, missing, surface_block, store_surface)
        if plan.wide > pairs:
            moved[t, pairs:, :] = jnp.zeros((plan.wide - pairs, 128), BF16)
        if t == 0:
            continue

        def schur_block(slot, t=t):
            return first[t][plan.schur_at :, :][plan.rows(slot), :].astype(F32)

        if t == plan.last:
            block = last_block(plan, missing[t], schur_block).astype(BF16)
        else:
            block = first[t][plan.schur_at :, :][plan.rows(t - 1), :]
        at = pairs + each * (t % 2)
        image = received[t][at : at + each, :].astype(F32)
        changes.append(image - dot(block, moved[t]))
    for slot in plan.slots():
        far_rows[plan.rows(slot), :] = jnp.where(
            missing[0] == slot + 1.0, changes[plan.last - 1], changes[slot]
        )
    if plan.wide > pairs:
        far_rows[pairs:, :] = jnp.zeros((plan.wide - pairs, 128), F32)
    far = far_image[...] - step * far_rows[...]
    place_v = place[...]
    weight = whole_weight(place_v)
    operated = surface[...].astype(F32) - dot(place_v, moved[0])
    remaining = residual[...] - step * operated
    image = dot(schur[...], (weight * remaining).astype(BF16)).astype(BF16)
    preconditioned[...] = weight * (image.astype(F32) - dot(place_v, far.astype(BF16)))
    last_copy = pltpu.make_async_copy(preconditioned, preconditioned_out, sent.at[1])
    last_copy.start()
    solution_copy.wait()
    last_copy.wait()


def line_body(
    plan,
    flexibility,
    dirichlet_schur,
    subdomain_loads,
    coupling,
    coarse_rows,
    neighbors,
    interface_rows,
    coarse_map,
):
    line, order = plan.line, plan.order
    coarse = coarse_rows[0, 0]
    rows = jnp.transpose(interface_rows, (0, 2, 1, 3))[0]
    whole = pl.BlockSpec(memory_space=pltpu.VMEM)
    outside = pl.BlockSpec(memory_space=pltpu.HBM)
    params = pltpu.CompilerParams(vmem_limit_bytes=VMEM_BYTES)

    def shape(*dims, kind=F32):
        return jax.ShapeDtypeStruct(dims, kind)

    def swap(value, axis, distance):
        size = lax.axis_size(axis)
        return lax.ppermute(value, axis, [(at, at ^ distance) for at in range(size)])

    def line_blocks(messages, riders=()):
        blocks = [messages[0]] + [None] * (line - 1)
        carried = []
        for far in reversed(range(2, line, 2)):
            blocks[far] = swap(messages[far // 2], "sub", far)
        blocks[1] = swap(messages[0], "sub", 1)
        for far in reversed(range(2, line, 2)):
            for rider, distance in riders[len(carried) : 0 if far > 2 else None]:
                blocks[far], rider = lax.optimization_barrier((blocks[far], rider))
                carried.append(swap(rider, "grp", distance))
            blocks[far + 1] = swap(blocks[far], "sub", 1)
        return blocks, carried

    lists = (neighbors[0], rows, coarse_map[0])
    kept = (dirichlet_schur[0, 0], subdomain_loads[0, 0], coupling[0, 0].T, flexibility[0, 0])
    inputs = [pltpu.with_memory_space_constraint(array, pltpu.HBM) for array in lists + kept]
    message, place, schur, loads, coupling_t, flex = pl.pallas_call(
        functools.partial(prepare_kernel, plan),
        out_shape=(shape(plan.first, 128, kind=BF16), shape(order, plan.wide, kind=BF16))
        + tuple(shape(*array.shape, kind=BF16) for array in kept),
        in_specs=[outside] * 7,
        out_specs=(whole,) * 6,
        scratch_shapes=[pltpu.VMEM(array.shape, array.dtype) for array in lists]
        + [
            pltpu.VMEM((round_up(plan.neighbors, 8), plan.wide), jnp.int32),
            pltpu.VMEM((8, 128), F32),
            pltpu.VMEM((plan.wide, order), BF16),
            pltpu.SemaphoreType.DMA((7,)),
        ],
        compiler_params=params,
        name="prepare",
    )(*inputs)
    riders = [(coarse, distance) for distance in reversed(range(1, plan.groups))]
    first, carried = line_blocks([message] * (line // 2), riders)
    coarse_all = [coarse] + carried[::-1]

    message, residual, direction, local_part, far_image = pl.pallas_call(
        functools.partial(direction_kernel, plan),
        out_shape=(
            shape(plan.second, 128, kind=BF16),
            shape(order, 128),
            shape(order, 128),
            shape(order, 128),
            shape(plan.wide, 128),
        ),
        in_specs=[whole] * (line + plan.groups + 4),
        out_specs=(whole,) * 5,
        scratch_shapes=[
            pltpu.VMEM((line, plan.wide, 128), BF16),
            pltpu.VMEM((line, plan.pairs, 128), F32),
            pltpu.VMEM((line, plan.pairs, 128), F32),
            pltpu.VMEM((line, plan.spread, 128), F32),
        ],
        compiler_params=params,
        name="direction",
    )(*first, *coarse_all, schur, flex, loads, place)
    heard = [message]
    for step in range(1, plan.groups):
        heard.append(swap(message, "grp", step))

    surface, *messages = pl.pallas_call(
        functools.partial(surface_kernel, plan),
        out_shape=(shape(order, 128, kind=BF16),)
        + (shape(plan.third, 128, kind=BF16),) * (line // 2),
        in_specs=[whole] * (plan.groups + 5),
        out_specs=(whole,) * (1 + line // 2),
        compiler_params=params,
        name="surface",
    )(*heard, first[0], schur, coupling_t, place, local_part)
    last, _ = line_blocks(messages)

    solved, preconditioned = pl.pallas_call(
        functools.partial(result_kernel, plan),
        out_shape=(shape(order, 128), shape(order, 128)),
        in_specs=[whole] * (2 * line + 6),
        out_specs=(outside, outside),
        scratch_shapes=[
            pltpu.VMEM((line, plan.wide, 128), BF16),
            pltpu.VMEM((plan.wide, 128), F32),
            pltpu.VMEM((order, 128), F32),
            pltpu.VMEM((order, 128), F32),
            pltpu.SemaphoreType.DMA((2,)),
        ],
        compiler_params=params,
        name="result",
    )(*last, *first, far_image, residual, direction, surface, schur, place)
    return solved[None, None], preconditioned[None, None]


def wide_body(
    flexibility,
    dirichlet_schur,
    subdomain_loads,
    coupling,
    coarse_rows,
    neighbors,
    interface_rows,
    coarse_map,
):
    flex_block = flexibility[0, 0]
    schur_block = dirichlet_schur[0, 0]
    loads_block = subdomain_loads[0, 0]
    couple_block = coupling[0, 0]
    coarse_block = coarse_rows[0, 0]
    neighbor_ids = neighbors[0, 0]
    row_lists = interface_rows[0, 0]
    corner_ids = coarse_map[0, 0]
    order_size = flex_block.shape[0]
    column_count = loads_block.shape[1]
    coarse_size = coarse_block.shape[1]
    line_size = lax.axis_size("sub")
    flat_rows = row_lists.reshape(-1)
    destinations = (
        jnp.arange(line_size, dtype=jnp.int32)[:, None] == neighbor_ids[None, :]
    ).astype(jnp.bfloat16)
    pair_mask = jnp.zeros((order_size,), jnp.float32).at[flat_rows].set(1.0)
    weight = (1.0 - 0.5 * pair_mask)[:, None]

    def jump_field(surface):
        picked = surface[flat_rows].reshape(row_lists.shape + (column_count,))
        outgoing = jnp.einsum(
            "dk,kjc->djc", destinations, picked, preferred_element_type=jnp.float32
        ).astype(jnp.bfloat16)
        incoming = lax.all_to_all(outgoing, "sub", split_axis=0, concat_axis=0, tiled=True)
        matched = jnp.einsum(
            "dk,djc->kjc", destinations, incoming, preferred_element_type=jnp.float32
        )
        placed = (
            jnp.zeros((order_size, column_count), jnp.float32)
            .at[flat_rows]
            .set(matched.reshape(-1, column_count))
        )
        return surface.astype(jnp.float32) - placed

    def precondition(residual):
        scaled = (weight * residual).astype(jnp.bfloat16)
        schur_image = jnp.dot(schur_block, scaled, preferred_element_type=jnp.float32).astype(
            jnp.bfloat16
        )
        return weight * jump_field(schur_image)

    def column_dot(first_field, second_field):
        return lax.psum(jnp.sum(weight * first_field * second_field, axis=0), ("sub", "grp"))

    residual = jump_field(loads_block)
    zfield = precondition(residual)
    direction = zfield
    inner = column_dot(residual, zfield)
    dir_half = direction.astype(jnp.bfloat16)
    local_part = jnp.dot(flex_block, dir_half, preferred_element_type=jnp.float32)
    coarse_in = jnp.dot(couple_block.T, dir_half, preferred_element_type=jnp.float32)
    dense_sum = jnp.zeros((coarse_size, column_count), jnp.float32).at[corner_ids].set(coarse_in)
    partial_rows = lax.psum_scatter(dense_sum, "grp", scatter_dimension=0, tiled=True)
    panel_half = lax.psum(partial_rows, "sub").astype(jnp.bfloat16)
    coarse_val = jnp.dot(
        coarse_block,
        lax.all_gather(panel_half, "grp", axis=0, tiled=True),
        preferred_element_type=jnp.float32,
    ).astype(jnp.bfloat16)
    surface = (
        local_part + jnp.dot(couple_block, coarse_val, preferred_element_type=jnp.float32)
    ).astype(jnp.bfloat16)
    operated = jump_field(surface)
    step_size = inner / column_dot(direction, operated)
    solution = step_size * direction
    residual = residual - step_size * operated
    zfield = precondition(residual)
    return (solution[None, None], zfield[None, None])


def body(*arrays):
    flexibility, _, loads, _, coarse_rows, neighbors, interface_rows, _ = arrays
    plan = Plan(
        line=lax.axis_size("sub"),
        groups=lax.axis_size("grp"),
        order=flexibility.shape[2],
        columns=loads.shape[3],
        corners=coarse_rows.shape[2],
        coarse=coarse_rows.shape[3],
        neighbors=neighbors.shape[2],
        each=interface_rows.shape[3],
    )
    if plan.served():
        return line_body(plan, *arrays)
    return wide_body(*arrays)


def solution(mesh):
    placed = (
        P("sub", "grp", None, None),
        P("sub", "grp", None, None),
        P("sub", "grp", None, None),
        P("sub", "grp", None, None),
        P("sub", "grp", None, None),
        P("sub", "grp", None),
        P("sub", "grp", None, None),
        P("sub", "grp", None),
    )
    return jax.shard_map(
        body,
        mesh=mesh,
        in_specs=placed,
        out_specs=(P("sub", "grp", None, None), P("sub", "grp", None, None)),
        check_vma=False,
    )
```

```python
import functools

import jax
import jax.numpy as jnp
from jax import lax
from jax.experimental import pallas as pl
from jax.experimental.pallas import tpu as pltpu
from jax.sharding import PartitionSpec as P

F32 = jnp.float32
BF16 = jnp.bfloat16
VMEM_BYTES = 24 * 1024 * 1024


def round_up(value, unit):
    return -(-value // unit) * unit


class Plan:
    def __init__(self, line, groups, order, columns, corners, coarse, neighbors, each):
        self.line, self.groups = line, groups
        self.order, self.columns = order, columns
        self.corners, self.coarse = corners, coarse
        self.neighbors, self.each = neighbors, each
        self.last = line - 1
        self.pairs = neighbors * each
        self.wide = round_up(self.pairs, 128)
        self.image_at = self.pairs
        self.schur_at = 2 * self.pairs
        self.coarse_at = 3 * self.pairs
        self.tail = round_up(2 * corners, 16)
        self.first = self.coarse_at + self.tail
        self.input_at = groups * corners
        self.dots_at = self.input_at + corners
        self.second = round_up(self.dots_at + 8, 16)
        self.sums_at = self.pairs + 2 * each
        self.third = self.sums_at + 16
        self.spread = round_up(corners, 32)

    def served(self):
        return (
            self.line >= 4
            and self.line & (self.line - 1) == 0
            and self.groups & (self.groups - 1) == 0
            and self.neighbors == self.line - 2
            and self.each % 16 == 0
            and self.columns == 128
            and self.wide == 128
            and self.pairs + self.corners <= 128
            and self.corners % 8 == 0
            and self.corners >= 8
            and 128 % self.spread == 0
            and (self.line * self.spread) % 128 == 0
            and self.order % 128 == 0
            and self.coarse % 128 == 0
            and self.coarse <= 128 * 256
        )

    def slots(self):
        return range(self.neighbors)

    def rows(self, slot):
        return slice(self.each * slot, self.each * (slot + 1))


def dot(a, b):
    return jnp.dot(a, b, preferred_element_type=F32)


def dot_over_rows(a, b):
    return lax.dot_general(a, b, (((0,), (0,)), ((), ())), preferred_element_type=F32)


def dot_over_lanes(a, b):
    return lax.dot_general(a, b, (((1,), (1,)), ((), ())), preferred_element_type=F32)


def split(value):
    high = value.astype(BF16).astype(F32)
    return high, value - high


def stack_rows(values, height):
    row = lax.broadcasted_iota(jnp.int32, (height, 128), 0)
    stacked = jnp.zeros((height, 128), F32)
    for at, value in enumerate(values):
        stacked = jnp.where(row == at, value, stacked)
    return stacked


def whole_weight(place):
    ones = jnp.ones((place.shape[1], 128), BF16)
    return 1.0 - 0.5 * dot(place, ones)


def missing_of(plan, tail):
    at = plan.corners + 2
    return jnp.broadcast_to(tail[at : at + 1, plan.pairs : plan.pairs + 1], (plan.each, 128))


def last_block(plan, missing, blocks):
    found = jnp.zeros((plan.each, 128), F32)
    for slot in plan.slots():
        found = jnp.where(missing == slot + 1.0, blocks(slot), found)
    return found


def gather_pairs(plan, t, missing, blocks, store):
    far = t ^ plan.last
    last = last_block(plan, missing[far], functools.partial(blocks, far))
    for slot in plan.slots():
        value = blocks(t ^ (slot + 1), slot)
        store(slot, jnp.where(missing[t] == slot + 1.0, last, value))


def prepare_kernel(
    plan,
    neighbors_in,
    rows_in,
    corner_map_in,
    schur_in,
    loads_in,
    coupling_in,
    flexibility_in,
    message,
    place,
    schur,
    loads,
    coupling_t,
    flexibility,
    neighbors,
    rows,
    corner_map,
    rows_pad,
    map_pad,
    couple_pad,
    arrived,
):
    me = lax.axis_index("sub")
    each, pairs, wide, corners = plan.each, plan.pairs, plan.wide, plan.corners
    sources = (neighbors_in, rows_in, corner_map_in, loads_in, coupling_in, schur_in)
    targets = (neighbors, rows, corner_map, loads, coupling_t, schur)
    sources += (flexibility_in,)
    targets += (flexibility,)
    copies = [
        pltpu.make_async_copy(source, target, arrived.at[at])
        for at, (source, target) in enumerate(zip(sources, targets))
    ]
    for copy in copies:
        copy.start()
    rows_pad[...] = jnp.zeros(rows_pad.shape, jnp.int32)
    map_pad[...] = jnp.zeros(map_pad.shape, F32)
    couple_pad[...] = jnp.zeros(couple_pad.shape, BF16)
    copies[0].wait()
    copies[1].wait()
    for k in range(plan.neighbors):
        rows_pad[k : k + 1, 0:each] = rows[k]
    spread = rows_pad[...]
    reach = each
    while reach < wide:
        spread = spread + pltpu.roll(spread, reach, 1)
        reach *= 2
    lane = lax.broadcasted_iota(jnp.int32, (1, wide), 1)
    distances = neighbors[...] ^ me
    missing = jnp.full((1, 1), plan.line * (plan.line - 1) // 2, jnp.int32)
    for k in range(plan.neighbors):
        missing = missing - distances[0:1, k : k + 1]
    index = jnp.full((1, wide), -1, jnp.int32)
    for k in range(plan.neighbors):
        distance = distances[0:1, k : k + 1]
        home = jnp.where(distance == plan.last, missing, distance)
        index = jnp.where(lane // each + 1 == home, spread[k : k + 1], index)
    wide_index = jnp.broadcast_to(index.astype(F32), (wide, wide))
    tall_index = wide_index.T.astype(jnp.int32)
    order_rows = lax.broadcasted_iota(jnp.int32, (plan.order, wide), 0)
    place_v = jnp.where(order_rows == index, 1.0, 0.0).astype(BF16)
    place[...] = place_v
    order_lanes = lax.broadcasted_iota(jnp.int32, (wide, plan.order), 1)
    pick_f = jnp.where(order_lanes == tall_index[:, 0:1], 1.0, 0.0)
    weight_row = 1.0 - 0.5 * jnp.sum(pick_f, axis=0, keepdims=True)
    pick = pick_f.astype(BF16)[:pairs]
    weight = whole_weight(place_v)
    copies[2].wait()
    corner_ids = corner_map[...]
    map_pad[0:1, 0:corners] = (corner_ids // 128).astype(F32)
    map_pad[1:2, 0:corners] = (corner_ids % 128).astype(F32)
    map_pad[2:3, :] = jnp.broadcast_to(missing.astype(F32), (1, 128))
    extra_lane = lax.broadcasted_iota(jnp.int32, (8, 128), 1)
    extra = jnp.where(extra_lane >= pairs, pltpu.roll(map_pad[...], pairs, 1), 0.0)
    copies[3].wait()
    load = loads[...]
    weighted = (weight * load.astype(F32)).astype(BF16)
    message[0:pairs, :] = dot(pick, load).astype(BF16)
    copies[4].wait()
    couple = coupling_t[...]
    couple_w = (couple.astype(F32) * weight_row).astype(BF16)
    room = round_up(corners, 16)
    padded = couple
    if room > corners:
        zeros = jnp.zeros((room - corners, plan.order), F32)
        padded = jnp.concatenate([couple.astype(F32), zeros], axis=0).astype(BF16)
    couple_pad[pairs : pairs + room, :] = padded
    edge = dot_over_lanes(pick, couple_pad[...])
    copies[5].wait()
    image = dot(schur[...], jnp.concatenate([weighted, place_v], axis=1)).astype(BF16)
    first = dot(pick, image)
    first_c = dot(couple_w, image)
    pair_part = 0.5 * first_c[:, 128:]
    tail = [first_c[:, :128], pair_part[:8] + extra]
    if corners > 8:
        tail.append(pair_part[8:])
    if plan.tail > 2 * corners:
        tail.append(jnp.zeros((plan.tail - 2 * corners, 128), F32))
    message[plan.image_at : plan.image_at + pairs, :] = first[:, :128].astype(BF16)
    message[plan.schur_at : plan.coarse_at, :] = (0.5 * (first[:, 128:] + edge)).astype(BF16)
    message[plan.coarse_at :, :] = jnp.concatenate(tail, axis=0).astype(BF16)
    copies[6].wait()


def direction_kernel(plan, *refs):
    line, pairs, corners = plan.line, plan.pairs, plan.corners
    received, refs = refs[:line], refs[line:]
    coarse_refs, refs = refs[: plan.groups], refs[plan.groups :]
    schur, flexibility, loads, place = refs[:4]
    message, residual, direction, local_part, far_image = refs[4:9]
    moved, images, moved_images, inputs = refs[9:]
    tails = [block[plan.coarse_at :, :].astype(F32) for block in received]
    missing = [missing_of(plan, tail) for tail in tails]
    codes = []
    per_tile = 128 // plan.spread
    lane = lax.broadcasted_iota(jnp.int32, (1, 128), 1)
    for first in range(0, line, per_tile):
        code = jnp.full((1, 128), -1, jnp.int32)
        for u in range(first, first + per_tile):
            number = pltpu.roll(tails[u][corners : corners + 8], 128 - pairs, 1)
            number = (128.0 * number[0:1] + number[1:2]).astype(jnp.int32)
            number = jnp.where(lane < corners, number, -1)
            code = jnp.maximum(code, pltpu.roll(number, (u - first) * plan.spread, 1))
        codes.append(code)
    codes = jnp.concatenate(codes, axis=1)
    coarse_rows = lax.broadcasted_iota(jnp.int32, (plan.coarse, codes.shape[1]), 0)
    chooser = jnp.where(coarse_rows == codes, 1.0, 0.0).astype(BF16)
    coarse_all = jnp.concatenate([ref[...] for ref in coarse_refs], axis=0)
    coarse_matrix = dot(coarse_all, chooser).astype(BF16)

    def loads_block(d, slot):
        return received[d][plan.rows(slot), :].astype(F32)

    def image_block(d, slot):
        return images[d, plan.rows(slot), :]

    changes = []
    for t in range(line):

        def store_loads(slot, value, t=t):
            moved[t, plan.rows(slot), :] = value.astype(BF16)

        gather_pairs(plan, t, missing, loads_block, store_loads)
        if plan.wide > pairs:
            moved[t, pairs:, :] = jnp.zeros((plan.wide - pairs, 128), BF16)
        result = dot(received[t][plan.schur_at :, :], moved[t])
        image = received[t][plan.image_at : plan.schur_at, :].astype(F32)
        images[t] = image - result[:pairs]
        changes.append(result[pairs + corners : pairs + 2 * corners])
    for t in range(line):

        def store_image(slot, value, t=t):
            moved_images[t, plan.rows(slot), :] = value

        gather_pairs(plan, t, missing, image_block, store_image)
        coupled = received[t][plan.schur_at : plan.coarse_at, :]
        edge = dot_over_rows(coupled, moved_images[t].astype(BF16))
        entry = tails[t][:corners] - changes[t] - edge[pairs : pairs + corners]
        parts = [entry]
        if plan.spread > corners:
            parts.append(jnp.zeros((plan.spread - corners, 128), F32))
        inputs[t] = jnp.concatenate(parts, axis=0)
    coarse_in = inputs[...].reshape(line * plan.spread, 128).astype(BF16)
    coarse_out = dot(coarse_matrix, coarse_in)

    place_v = place[...]
    weight = whole_weight(place_v)
    right = loads[...].astype(F32) - dot(place_v, moved[0])
    image = dot(schur[...], (weight * right).astype(BF16)).astype(BF16)
    mine = moved_images[0]
    if plan.wide > pairs:
        mine = jnp.concatenate([mine, jnp.zeros((plan.wide - pairs, 128), F32)], axis=0)
    far_image[...] = mine
    field = weight * (image.astype(F32) - dot(place_v, mine.astype(BF16)))
    residual[...] = right
    direction[...] = field
    local = dot(flexibility[...], field.astype(BF16))
    local_part[...] = local
    inner = split(jnp.sum(weight * right * field, axis=0, keepdims=True))
    square = split(jnp.sum(field * local, axis=0, keepdims=True))
    parts = [coarse_out, inputs[0][:corners], stack_rows(inner + square, 8)]
    if plan.second > plan.dots_at + 8:
        parts.append(jnp.zeros((plan.second - plan.dots_at - 8, 128), F32))
    message[...] = jnp.concatenate(parts, axis=0).astype(BF16)


def surface_kernel(plan, *refs):
    groups, corners, pairs = plan.groups, plan.corners, plan.pairs
    heard = [ref[...].astype(F32) for ref in refs[:groups]]
    own_first, schur, coupling_t, place, local_part = refs[groups : groups + 5]
    surface, messages = refs[groups + 5], refs[groups + 6 :]
    dots = sum(block[plan.dots_at : plan.dots_at + 8] for block in heard)
    inner = dots[0:1] + dots[1:2]
    square = dots[2:3] + dots[3:4]
    own = None
    for m in range(groups):
        value = 0.0
        for d in range(groups):
            at = corners * (m ^ d)
            value = value + heard[d][at : at + corners]
        value = value.astype(BF16)
        if m == 0:
            own = value
        entry = heard[m][plan.input_at : plan.input_at + corners]
        square = square + jnp.sum(entry * value.astype(F32), axis=0, keepdims=True)
    field = (local_part[...] + dot_over_rows(coupling_t[...], own)).astype(BF16)
    surface[...] = field
    place_v = place[...]
    weight = whole_weight(place_v)
    scaled = (weight * field.astype(F32)).astype(BF16)
    image = dot(schur[...], scaled).astype(BF16)
    both = dot_over_rows(place_v, jnp.concatenate([field, image], axis=1))[:pairs]
    surface_part = both[:, :128].astype(BF16)
    sums = stack_rows(split(inner) + split(square), 16).astype(BF16)
    missing = missing_of(plan, own_first[plan.coarse_at :, :].astype(F32))

    def image_part(distance):
        if distance == 0:
            return jnp.zeros((plan.each, 128), F32)
        if distance == plan.last:
            return last_block(plan, missing, lambda slot: image_part(slot + 1))
        return both[plan.rows(distance - 1), 128:]

    for far, message in zip(range(0, plan.line, 2), messages):
        message[0:pairs, :] = surface_part
        message[pairs : pairs + plan.each, :] = image_part(far).astype(BF16)
        message[pairs + plan.each : plan.sums_at, :] = image_part(far + 1).astype(BF16)
        message[plan.sums_at :, :] = sums


def result_kernel(plan, *refs):
    line, pairs, each = plan.line, plan.pairs, plan.each
    received, first, refs = refs[:line], refs[line : 2 * line], refs[2 * line :]
    far_image, residual, direction, surface, schur, place = refs[:6]
    solution_out, preconditioned_out = refs[6:8]
    moved, far_rows, solved, preconditioned, sent = refs[8:]
    sums = 0.0
    for block in received:
        sums = sums + block[plan.sums_at :, :].astype(F32)
    step = (sums[0:1] + sums[1:2]) / (sums[2:3] + sums[3:4])
    solved[...] = step * direction[...]
    solution_copy = pltpu.make_async_copy(solved, solution_out, sent.at[0])
    solution_copy.start()
    missing = [missing_of(plan, block[plan.coarse_at :, :].astype(F32)) for block in first]

    def surface_block(d, slot):
        return received[d][plan.rows(slot), :].astype(F32)

    changes = []
    for t in range(line):

        def store_surface(slot, value, t=t):
            moved[t, plan.rows(slot), :] = value.astype(BF16)

        gather_pairs(plan, t, missing, surface_block, store_surface)
        if plan.wide > pairs:
            moved[t, pairs:, :] = jnp.zeros((plan.wide - pairs, 128), BF16)
        if t == 0:
            continue

        def schur_block(slot, t=t):
            return first[t][plan.schur_at :, :][plan.rows(slot), :].astype(F32)

        if t == plan.last:
            block = last_block(plan, missing[t], schur_block).astype(BF16)
        else:
            block = first[t][plan.schur_at :, :][plan.rows(t - 1), :]
        at = pairs + each * (t % 2)
        image = received[t][at : at + each, :].astype(F32)
        changes.append(image - dot(block, moved[t]))
    for slot in plan.slots():
        far_rows[plan.rows(slot), :] = jnp.where(
            missing[0] == slot + 1.0, changes[plan.last - 1], changes[slot]
        )
    if plan.wide > pairs:
        far_rows[pairs:, :] = jnp.zeros((plan.wide - pairs, 128), F32)
    far = far_image[...] - step * far_rows[...]
    place_v = place[...]
    weight = whole_weight(place_v)
    operated = surface[...].astype(F32) - dot(place_v, moved[0])
    remaining = residual[...] - step * operated
    image = dot(schur[...], (weight * remaining).astype(BF16)).astype(BF16)
    preconditioned[...] = weight * (image.astype(F32) - dot(place_v, far.astype(BF16)))
    last_copy = pltpu.make_async_copy(preconditioned, preconditioned_out, sent.at[1])
    last_copy.start()
    solution_copy.wait()
    last_copy.wait()


def line_body(
    plan,
    flexibility,
    dirichlet_schur,
    subdomain_loads,
    coupling,
    coarse_rows,
    neighbors,
    interface_rows,
    coarse_map,
):
    line, order = plan.line, plan.order
    coarse = coarse_rows[0, 0]
    rows = jnp.transpose(interface_rows, (0, 2, 1, 3))[0]
    whole = pl.BlockSpec(memory_space=pltpu.VMEM)
    outside = pl.BlockSpec(memory_space=pltpu.HBM)
    params = pltpu.CompilerParams(vmem_limit_bytes=VMEM_BYTES)

    def shape(*dims, kind=F32):
        return jax.ShapeDtypeStruct(dims, kind)

    def swap(value, axis, distance):
        size = lax.axis_size(axis)
        return lax.ppermute(value, axis, [(at, at ^ distance) for at in range(size)])

    def line_blocks(messages, riders=()):
        blocks = [messages[0]] + [None] * (line - 1)
        carried = []
        for far in reversed(range(2, line, 2)):
            blocks[far] = swap(messages[far // 2], "sub", far)
        blocks[1] = swap(messages[0], "sub", 1)
        for far in reversed(range(2, line, 2)):
            blocks[far + 1] = swap(blocks[far], "sub", 1)
        for rider, distance in riders:
            rider = lax.optimization_barrier([rider] + [blocks[k] for k in (1,)])[0]
            carried.append(swap(rider, "grp", distance))
        return blocks, carried

    lists = (neighbors[0], rows, coarse_map[0])
    kept = (dirichlet_schur[0, 0], subdomain_loads[0, 0], coupling[0, 0].T, flexibility[0, 0])
    inputs = [pltpu.with_memory_space_constraint(array, pltpu.HBM) for array in lists + kept]
    message, place, schur, loads, coupling_t, flex = pl.pallas_call(
        functools.partial(prepare_kernel, plan),
        out_shape=(shape(plan.first, 128, kind=BF16), shape(order, plan.wide, kind=BF16))
        + tuple(shape(*array.shape, kind=BF16) for array in kept),
        in_specs=[outside] * 7,
        out_specs=(whole,) * 6,
        scratch_shapes=[pltpu.VMEM(array.shape, array.dtype) for array in lists]
        + [
            pltpu.VMEM((round_up(plan.neighbors, 8), plan.wide), jnp.int32),
            pltpu.VMEM((8, 128), F32),
            pltpu.VMEM((plan.wide, order), BF16),
            pltpu.SemaphoreType.DMA((7,)),
        ],
        compiler_params=params,
        name="prepare",
    )(*inputs)
    riders = [(coarse, distance) for distance in reversed(range(1, plan.groups))]
    first, carried = line_blocks([message] * (line // 2), riders)
    coarse_all = [coarse] + carried[::-1]

    message, residual, direction, local_part, far_image = pl.pallas_call(
        functools.partial(direction_kernel, plan),
        out_shape=(
            shape(plan.second, 128, kind=BF16),
            shape(order, 128),
            shape(order, 128),
            shape(order, 128),
            shape(plan.wide, 128),
        ),
        in_specs=[whole] * (line + plan.groups + 4),
        out_specs=(whole,) * 5,
        scratch_shapes=[
            pltpu.VMEM((line, plan.wide, 128), BF16),
            pltpu.VMEM((line, plan.pairs, 128), F32),
            pltpu.VMEM((line, plan.pairs, 128), F32),
            pltpu.VMEM((line, plan.spread, 128), F32),
        ],
        compiler_params=params,
        name="direction",
    )(*first, *coarse_all, schur, flex, loads, place)
    heard = [message]
    for step in range(1, plan.groups):
        heard.append(swap(message, "grp", step))

    surface, *messages = pl.pallas_call(
        functools.partial(surface_kernel, plan),
        out_shape=(shape(order, 128, kind=BF16),)
        + (shape(plan.third, 128, kind=BF16),) * (line // 2),
        in_specs=[whole] * (plan.groups + 5),
        out_specs=(whole,) * (1 + line // 2),
        compiler_params=params,
        name="surface",
    )(*heard, first[0], schur, coupling_t, place, local_part)
    last, _ = line_blocks(messages)

    solved, preconditioned = pl.pallas_call(
        functools.partial(result_kernel, plan),
        out_shape=(shape(order, 128), shape(order, 128)),
        in_specs=[whole] * (2 * line + 6),
        out_specs=(outside, outside),
        scratch_shapes=[
            pltpu.VMEM((line, plan.wide, 128), BF16),
            pltpu.VMEM((plan.wide, 128), F32),
            pltpu.VMEM((order, 128), F32),
            pltpu.VMEM((order, 128), F32),
            pltpu.SemaphoreType.DMA((2,)),
        ],
        compiler_params=params,
        name="result",
    )(*last, *first, far_image, residual, direction, surface, schur, place)
    return solved[None, None], preconditioned[None, None]


def wide_body(
    flexibility,
    dirichlet_schur,
    subdomain_loads,
    coupling,
    coarse_rows,
    neighbors,
    interface_rows,
    coarse_map,
):
    flex_block = flexibility[0, 0]
    schur_block = dirichlet_schur[0, 0]
    loads_block = subdomain_loads[0, 0]
    couple_block = coupling[0, 0]
    coarse_block = coarse_rows[0, 0]
    neighbor_ids = neighbors[0, 0]
    row_lists = interface_rows[0, 0]
    corner_ids = coarse_map[0, 0]
    order_size = flex_block.shape[0]
    column_count = loads_block.shape[1]
    coarse_size = coarse_block.shape[1]
    line_size = lax.axis_size("sub")
    flat_rows = row_lists.reshape(-1)
    destinations = (
        jnp.arange(line_size, dtype=jnp.int32)[:, None] == neighbor_ids[None, :]
    ).astype(jnp.bfloat16)
    pair_mask = jnp.zeros((order_size,), jnp.float32).at[flat_rows].set(1.0)
    weight = (1.0 - 0.5 * pair_mask)[:, None]

    def jump_field(surface):
        picked = surface[flat_rows].reshape(row_lists.shape + (column_count,))
        outgoing = jnp.einsum(
            "dk,kjc->djc", destinations, picked, preferred_element_type=jnp.float32
        ).astype(jnp.bfloat16)
        incoming = lax.all_to_all(outgoing, "sub", split_axis=0, concat_axis=0, tiled=True)
        matched = jnp.einsum(
            "dk,djc->kjc", destinations, incoming, preferred_element_type=jnp.float32
        )
        placed = (
            jnp.zeros((order_size, column_count), jnp.float32)
            .at[flat_rows]
            .set(matched.reshape(-1, column_count))
        )
        return surface.astype(jnp.float32) - placed

    def precondition(residual):
        scaled = (weight * residual).astype(jnp.bfloat16)
        schur_image = jnp.dot(schur_block, scaled, preferred_element_type=jnp.float32).astype(
            jnp.bfloat16
        )
        return weight * jump_field(schur_image)

    def column_dot(first_field, second_field):
        return lax.psum(jnp.sum(weight * first_field * second_field, axis=0), ("sub", "grp"))

    residual = jump_field(loads_block)
    zfield = precondition(residual)
    direction = zfield
    inner = column_dot(residual, zfield)
    dir_half = direction.astype(jnp.bfloat16)
    local_part = jnp.dot(flex_block, dir_half, preferred_element_type=jnp.float32)
    coarse_in = jnp.dot(couple_block.T, dir_half, preferred_element_type=jnp.float32)
    dense_sum = jnp.zeros((coarse_size, column_count), jnp.float32).at[corner_ids].set(coarse_in)
    partial_rows = lax.psum_scatter(dense_sum, "grp", scatter_dimension=0, tiled=True)
    panel_half = lax.psum(partial_rows, "sub").astype(jnp.bfloat16)
    coarse_val = jnp.dot(
        coarse_block,
        lax.all_gather(panel_half, "grp", axis=0, tiled=True),
        preferred_element_type=jnp.float32,
    ).astype(jnp.bfloat16)
    surface = (
        local_part + jnp.dot(couple_block, coarse_val, preferred_element_type=jnp.float32)
    ).astype(jnp.bfloat16)
    operated = jump_field(surface)
    step_size = inner / column_dot(direction, operated)
    solution = step_size * direction
    residual = residual - step_size * operated
    zfield = precondition(residual)
    return (solution[None, None], zfield[None, None])


def body(*arrays):
    flexibility, _, loads, _, coarse_rows, neighbors, interface_rows, _ = arrays
    plan = Plan(
        line=lax.axis_size("sub"),
        groups=lax.axis_size("grp"),
        order=flexibility.shape[2],
        columns=loads.shape[3],
        corners=coarse_rows.shape[2],
        coarse=coarse_rows.shape[3],
        neighbors=neighbors.shape[2],
        each=interface_rows.shape[3],
    )
    if plan.served():
        return line_body(plan, *arrays)
    return wide_body(*arrays)


def solution(mesh):
    placed = (
        P("sub", "grp", None, None),
        P("sub", "grp", None, None),
        P("sub", "grp", None, None),
        P("sub", "grp", None, None),
        P("sub", "grp", None, None),
        P("sub", "grp", None),
        P("sub", "grp", None, None),
        P("sub", "grp", None),
    )
    return jax.shard_map(
        body,
        mesh=mesh,
        in_specs=placed,
        out_specs=(P("sub", "grp", None, None), P("sub", "grp", None, None)),
        check_vma=False,
    )
```

```python
import functools

import jax
import jax.numpy as jnp
from jax import lax
from jax.experimental import pallas as pl
from jax.experimental.pallas import tpu as pltpu
from jax.sharding import PartitionSpec as P

F32 = jnp.float32
BF16 = jnp.bfloat16
VMEM_BYTES = 24 * 1024 * 1024


def round_up(value, unit):
    return -(-value // unit) * unit


class Plan:
    def __init__(self, line, groups, order, columns, corners, coarse, neighbors, each):
        self.line, self.groups = line, groups
        self.order, self.columns = order, columns
        self.corners, self.coarse = corners, coarse
        self.neighbors, self.each = neighbors, each
        self.last = line - 1
        self.pairs = neighbors * each
        self.wide = round_up(self.pairs, 128)
        self.half = self.pairs // 2
        self.spare = 128 - self.pairs
        self.map_lane = self.pairs + self.half - self.spare
        self.image_at = self.pairs
        self.schur_at = 2 * self.pairs
        self.edge_at = self.schur_at + self.half
        self.coarse_at = self.edge_at + self.half
        self.first = self.coarse_at + corners
        self.input_at = groups * corners
        self.dots_at = self.input_at + corners
        self.second = round_up(self.dots_at + 8, 16)
        self.sums_at = self.pairs + 2 * each
        self.third = self.sums_at + 16
        self.spread = round_up(corners, 32)

    def served(self):
        return (
            self.line >= 4
            and self.line & (self.line - 1) == 0
            and self.groups & (self.groups - 1) == 0
            and self.neighbors == self.line - 2
            and self.each % 16 == 0
            and self.columns == 128
            and self.wide == 128
            and self.pairs % 32 == 0
            and self.spare <= self.half < 2 * self.spare
            and 2 * self.corners == self.half
            and self.corners <= 2 * (128 - self.map_lane)
            and self.corners % 8 == 0
            and 128 % self.spread == 0
            and (self.line * self.spread) % 128 == 0
            and self.order % 128 == 0
            and self.coarse % 128 == 0
            and self.coarse <= 128 * 256
        )

    def slots(self):
        return range(self.neighbors)

    def rows(self, slot):
        return slice(self.each * slot, self.each * (slot + 1))


def dot(a, b):
    return jnp.dot(a, b, preferred_element_type=F32)


def dot_over_rows(a, b):
    return lax.dot_general(a, b, (((0,), (0,)), ((), ())), preferred_element_type=F32)


def dot_over_lanes(a, b):
    return lax.dot_general(a, b, (((1,), (1,)), ((), ())), preferred_element_type=F32)


def split(value):
    high = value.astype(BF16).astype(F32)
    return high, value - high


def stack_rows(values, height):
    row = lax.broadcasted_iota(jnp.int32, (height, 128), 0)
    stacked = jnp.zeros((height, 128), F32)
    for at, value in enumerate(values):
        stacked = jnp.where(row == at, value, stacked)
    return stacked


def whole_weight(place):
    ones = jnp.ones((place.shape[1], 128), BF16)
    return 1.0 - 0.5 * dot(place, ones)


def extra_rows(plan, values, missing):
    room = 128 - plan.map_lane
    lane = lax.broadcasted_iota(jnp.int32, (8, 128), 1)
    near = pltpu.roll(values, plan.map_lane, 1)
    far = pltpu.roll(values, plan.map_lane - room, 1)
    rows = [near[0:1], far[0:1], near[1:2], far[1:2], jnp.broadcast_to(missing, (1, 128))]
    return jnp.where(lane >= plan.map_lane, stack_rows(rows, 8), 0.0)


def map_rows(plan, extra):
    room = 128 - plan.map_lane
    lane = lax.broadcasted_iota(jnp.int32, (1, 128), 1)
    near = pltpu.roll(extra, room, 1)
    far = pltpu.roll(extra, 2 * room, 1)
    return [jnp.where(lane < room, near[at : at + 1], far[at + 1 : at + 2]) for at in (0, 2)]


def missing_of(plan, extra):
    return jnp.broadcast_to(extra[4:5, plan.map_lane : plan.map_lane + 1], (plan.each, 128))


def last_block(plan, missing, blocks):
    found = jnp.zeros((plan.each, 128), F32)
    for slot in plan.slots():
        found = jnp.where(missing == slot + 1.0, blocks(slot), found)
    return found


def gather_pairs(plan, t, missing, blocks, store):
    far = t ^ plan.last
    last = last_block(plan, missing[far], functools.partial(blocks, far))
    for slot in plan.slots():
        value = blocks(t ^ (slot + 1), slot)
        store(slot, jnp.where(missing[t] == slot + 1.0, last, value))


def prepare_kernel(
    plan,
    neighbors_in,
    rows_in,
    corner_map_in,
    schur_in,
    loads_in,
    coupling_in,
    flexibility_in,
    message,
    place,
    weight_out,
    schur_place,
    schur,
    loads,
    coupling_t,
    flexibility,
    neighbors,
    rows,
    corner_map,
    rows_pad,
    map_pad,
    arrived,
):
    me = lax.axis_index("sub")
    each, pairs, wide, corners = plan.each, plan.pairs, plan.wide, plan.corners
    sources = (neighbors_in, rows_in, corner_map_in, loads_in, coupling_in, schur_in)
    targets = (neighbors, rows, corner_map, loads, coupling_t, schur)
    sources += (flexibility_in,)
    targets += (flexibility,)
    copies = [
        pltpu.make_async_copy(source, target, arrived.at[at])
        for at, (source, target) in enumerate(zip(sources, targets))
    ]
    for copy in copies:
        copy.start()
    rows_pad[...] = jnp.zeros(rows_pad.shape, jnp.int32)
    map_pad[...] = jnp.zeros(map_pad.shape, F32)
    copies[0].wait()
    copies[1].wait()
    for k in range(plan.neighbors):
        rows_pad[k : k + 1, 0:each] = rows[k]
    spread = rows_pad[...]
    reach = each
    while reach < wide:
        spread = spread + pltpu.roll(spread, reach, 1)
        reach *= 2
    lane = lax.broadcasted_iota(jnp.int32, (1, wide), 1)
    distances = neighbors[...] ^ me
    missing = jnp.full((1, 1), plan.line * (plan.line - 1) // 2, jnp.int32)
    for k in range(plan.neighbors):
        missing = missing - distances[0:1, k : k + 1]
    index = jnp.full((1, wide), -1, jnp.int32)
    for k in range(plan.neighbors):
        distance = distances[0:1, k : k + 1]
        home = jnp.where(distance == plan.last, missing, distance)
        index = jnp.where(lane // each + 1 == home, spread[k : k + 1], index)
    wide_index = jnp.broadcast_to(index.astype(F32), (wide, wide))
    tall_index = wide_index.T.astype(jnp.int32)
    order_rows = lax.broadcasted_iota(jnp.int32, (plan.order, wide), 0)
    place_v = jnp.where(order_rows == index, 1.0, 0.0).astype(BF16)
    place[...] = place_v
    order_lanes = lax.broadcasted_iota(jnp.int32, (wide, plan.order), 1)
    pick_f = jnp.where(order_lanes == tall_index[:, 0:1], 1.0, 0.0)
    weight_row = 1.0 - 0.5 * jnp.sum(pick_f, axis=0, keepdims=True)
    pick = pick_f.astype(BF16)[:pairs]
    weight = whole_weight(place_v)
    weight_out[...] = weight.astype(BF16)
    copies[2].wait()
    corner_ids = corner_map[...]
    map_pad[0:1, 0:corners] = (corner_ids // 128).astype(F32)
    map_pad[1:2, 0:corners] = (corner_ids % 128).astype(F32)
    extra = extra_rows(plan, map_pad[...], missing.astype(F32))
    copies[3].wait()
    load = loads[...]
    weighted = (weight * load.astype(F32)).astype(BF16)
    message[0:pairs, :] = dot(pick, load).astype(BF16)
    copies[4].wait()
    couple = coupling_t[...]
    couple_w = couple.astype(F32) * weight_row
    edge = dot(couple, place_v)
    copies[5].wait()
    image = dot(schur[...], jnp.concatenate([weighted, place_v], axis=1))
    schur_place[...] = (0.5 * image[:, 128:]).astype(BF16)
    image = image.astype(BF16)
    picks = jnp.concatenate([pick_f[:pairs], couple_w], axis=0).astype(BF16)
    first = dot(picks, image)
    first, first_c = first[:pairs], first[pairs:]
    half, spare = plan.half, plan.spare
    lane = lax.broadcasted_iota(jnp.int32, (half, 128), 1)
    block = 0.5 * first[:, 128:]
    upper, quarter = block[:half], block[half:]
    upper = jnp.where(lane < pairs, upper, pltpu.roll(quarter, pairs - half, 1))
    coarse_part = 0.5 * jnp.concatenate([first_c[:, 128:], edge], axis=0)
    rest = jnp.where(lane < plan.map_lane, pltpu.roll(quarter, pairs - half - spare, 1), 0.0)
    coarse_part = jnp.where(lane < pairs, coarse_part, rest)
    coarse_part = jnp.concatenate([coarse_part[:8] + extra, coarse_part[8:]], axis=0)
    message[plan.image_at : plan.image_at + pairs, :] = first[:, :128].astype(BF16)
    message[plan.schur_at : plan.edge_at, :] = upper.astype(BF16)
    message[plan.edge_at : plan.coarse_at, :] = coarse_part.astype(BF16)
    message[plan.coarse_at :, :] = first_c[:, :128].astype(BF16)
    copies[6].wait()


def direction_kernel(plan, *refs):
    line, pairs, corners = plan.line, plan.pairs, plan.corners
    received, refs = refs[:line], refs[line:]
    coarse_refs, refs = refs[: plan.groups], refs[plan.groups :]
    schur, flexibility, loads, place, weight = refs[:5]
    message, image_out, direction, local_part, far_image, schur_rows, missing_out = refs[5:12]
    moved, images, moved_images, inputs, products = refs[12:]
    half, spare = plan.half, plan.spare
    extras = [block[plan.edge_at : plan.edge_at + 16, :].astype(F32) for block in received]
    missing = [missing_of(plan, extra) for extra in extras]
    missing_out[...] = stack_rows([value[0:1] for value in missing], line)
    codes = []
    per_tile = 128 // plan.spread
    lane = lax.broadcasted_iota(jnp.int32, (1, 128), 1)
    for first in range(0, line, per_tile):
        code = jnp.full((1, 128), -1, jnp.int32)
        for u in range(first, first + per_tile):
            high, low = map_rows(plan, extras[u][:8])
            number = (128.0 * high + low).astype(jnp.int32)
            number = jnp.where(lane < corners, number, -1)
            code = jnp.maximum(code, pltpu.roll(number, (u - first) * plan.spread, 1))
        codes.append(code)
    codes = jnp.concatenate(codes, axis=1)
    coarse_rows = lax.broadcasted_iota(jnp.int32, (plan.coarse, codes.shape[1]), 0)
    chooser = jnp.where(coarse_rows == codes, 1.0, 0.0).astype(BF16)
    coarse_all = jnp.concatenate([ref[...] for ref in coarse_refs], axis=0)
    coarse_matrix = dot(coarse_all, chooser).astype(BF16)

    def loads_block(d, slot):
        return received[d][plan.rows(slot), :].astype(F32)

    def image_block(d, slot):
        return images[d, plan.rows(slot), :]

    changes = []
    for t in range(line):

        def store_loads(slot, value, t=t):
            moved[t, plan.rows(slot), :] = value.astype(BF16)

        gather_pairs(plan, t, missing, loads_block, store_loads)
        if plan.wide > pairs:
            moved[t, pairs:, :] = jnp.zeros((plan.wide - pairs, 128), BF16)
        upper = received[t][plan.schur_at : plan.edge_at, :]
        coarse_part = received[t][plan.edge_at : plan.coarse_at, :]
        upper_f, coarse_f = upper.astype(F32), coarse_part.astype(F32)
        blank = jnp.zeros((128 - half, 128), F32)
        turned = jnp.concatenate([upper_f, blank], axis=0).T[half:pairs]
        near = pltpu.roll(upper_f, 128 - pairs + half, 1)
        far = pltpu.roll(coarse_f, 128 - pairs + half + spare, 1)
        lower = jnp.where(lane < half + spare, near, far)
        lower = jnp.where(lane < half, turned, jnp.where(lane < pairs, lower, 0.0))
        products[t, 0:half, :] = upper
        products[t, half:pairs, :] = lower.astype(BF16)
        products[t, pairs:, :] = coarse_part
        result = dot(products[t], moved[t])
        image = received[t][plan.image_at : plan.schur_at, :].astype(F32)
        images[t] = image - result[:pairs]
        changes.append(result[pairs : pairs + corners])
    for t in range(line):

        def store_image(slot, value, t=t):
            moved_images[t, plan.rows(slot), :] = value

        gather_pairs(plan, t, missing, image_block, store_image)
        if plan.wide > pairs:
            moved_images[t, pairs:, :] = jnp.zeros((plan.wide - pairs, 128), F32)
        edge = dot(products[t, pairs:, :], moved_images[t].astype(BF16))
        coarse_part = received[t][plan.coarse_at :, :].astype(F32)
        entry = coarse_part - changes[t] - edge[corners:]
        parts = [entry]
        if plan.spread > corners:
            parts.append(jnp.zeros((plan.spread - corners, 128), F32))
        inputs[t] = jnp.concatenate(parts, axis=0)
    coarse_in = inputs[...].reshape(line * plan.spread, 128).astype(BF16)
    coarse_out = dot(coarse_matrix, coarse_in)

    place_v = place[...]
    weight = weight[...].astype(F32)
    right = loads[...].astype(F32) - dot(place_v, moved[0])
    image = dot(schur[...], (weight * right).astype(BF16))
    image_out[...] = image
    image = image.astype(BF16)
    for t in range(1, line):
        if t < plan.last:
            rows = products[t, plan.rows(t - 1), :]
        else:
            rows = last_block(
                plan, missing[t], lambda slot: products[plan.last, plan.rows(slot), :].astype(F32)
            ).astype(BF16)
        schur_rows[plan.rows(t - 1), :] = rows
    mine = moved_images[0]
    far_image[...] = mine
    field = weight * (image.astype(F32) - dot(place_v, mine.astype(BF16)))
    direction[...] = field
    local = dot(flexibility[...], field.astype(BF16))
    local_part[...] = local
    inner = split(jnp.sum(weight * right * field, axis=0, keepdims=True))
    square = split(jnp.sum(field * local, axis=0, keepdims=True))
    parts = [coarse_out, inputs[0][:corners], stack_rows(inner + square, 8)]
    if plan.second > plan.dots_at + 8:
        parts.append(jnp.zeros((plan.second - plan.dots_at - 8, 128), F32))
    message[...] = jnp.concatenate(parts, axis=0).astype(BF16)


def surface_kernel(plan, *refs):
    groups, corners, pairs = plan.groups, plan.corners, plan.pairs
    heard = [ref[...].astype(F32) for ref in refs[:groups]]
    missing_rows, schur, coupling_t, place, weight, local_part = refs[groups : groups + 6]
    image_out, messages = refs[groups + 6], refs[groups + 7 :]
    dots = sum(block[plan.dots_at : plan.dots_at + 8] for block in heard)
    inner = dots[0:1] + dots[1:2]
    square = dots[2:3] + dots[3:4]
    own = None
    for m in range(groups):
        value = 0.0
        for d in range(groups):
            at = corners * (m ^ d)
            value = value + heard[d][at : at + corners]
        value = value.astype(BF16)
        if m == 0:
            own = value
        entry = heard[m][plan.input_at : plan.input_at + corners]
        square = square + jnp.sum(entry * value.astype(F32), axis=0, keepdims=True)
    field = (local_part[...] + dot_over_rows(coupling_t[...], own)).astype(BF16)
    scaled = (weight[...].astype(F32) * field.astype(F32)).astype(BF16)
    image = dot(schur[...], scaled)
    image_out[...] = image
    both = jnp.concatenate([field, image.astype(BF16)], axis=1)
    both = dot_over_rows(place[...], both)[:pairs]
    surface_part = both[:, :128].astype(BF16)
    sums = stack_rows(split(inner) + split(square), 16).astype(BF16)
    missing = jnp.broadcast_to(missing_rows[0:1, :], (plan.each, 128))

    def image_part(distance):
        if distance == 0:
            return jnp.zeros((plan.each, 128), F32)
        if distance == plan.last:
            return last_block(plan, missing, lambda slot: image_part(slot + 1))
        return both[plan.rows(distance - 1), 128:]

    for far, message in zip(range(0, plan.line, 2), messages):
        message[0:pairs, :] = surface_part
        message[pairs : pairs + plan.each, :] = image_part(far).astype(BF16)
        message[pairs + plan.each : plan.sums_at, :] = image_part(far + 1).astype(BF16)
        message[plan.sums_at :, :] = sums


def result_kernel(plan, *refs):
    line, pairs, each = plan.line, plan.pairs, plan.each
    received, schur_rows, missing_rows, refs = refs[:line], refs[line], refs[line + 1], refs[line + 2 :]
    far_image, first_image, direction, surface_image, schur_place, place, weight = refs[:7]
    solution_out, preconditioned_out = refs[7:9]
    moved, far_rows, solved, preconditioned, sent = refs[9:]
    sums = 0.0
    for block in received:
        sums = sums + block[plan.sums_at :, :].astype(F32)
    step = (sums[0:1] + sums[1:2]) / (sums[2:3] + sums[3:4])
    solved[...] = step * direction[...]
    solution_copy = pltpu.make_async_copy(solved, solution_out, sent.at[0])
    solution_copy.start()
    missing = [jnp.broadcast_to(missing_rows[t : t + 1, :], (each, 128)) for t in range(line)]

    def surface_block(d, slot):
        return received[d][plan.rows(slot), :].astype(F32)

    changes = []
    for t in range(line):

        def store_surface(slot, value, t=t):
            moved[t, plan.rows(slot), :] = value.astype(BF16)

        gather_pairs(plan, t, missing, surface_block, store_surface)
        if plan.wide > pairs:
            moved[t, pairs:, :] = jnp.zeros((plan.wide - pairs, 128), BF16)
        if t == 0:
            continue

        block = schur_rows[plan.rows(t - 1), :]
        at = pairs + each * (t % 2)
        image = received[t][at : at + each, :].astype(F32)
        changes.append(image - dot(block, moved[t]))
    for slot in plan.slots():
        far_rows[plan.rows(slot), :] = jnp.where(
            missing[0] == slot + 1.0, changes[plan.last - 1], changes[slot]
        )
    if plan.wide > pairs:
        far_rows[pairs:, :] = jnp.zeros((plan.wide - pairs, 128), F32)
    far = far_image[...] - step * far_rows[...]
    change = surface_image[...] - dot(schur_place[...], moved[0])
    remaining = first_image[...] - step * change - dot(place[...], far.astype(BF16))
    preconditioned[...] = weight[...].astype(F32) * remaining
    last_copy = pltpu.make_async_copy(preconditioned, preconditioned_out, sent.at[1])
    last_copy.start()
    solution_copy.wait()
    last_copy.wait()


def line_body(
    plan,
    flexibility,
    dirichlet_schur,
    subdomain_loads,
    coupling,
    coarse_rows,
    neighbors,
    interface_rows,
    coarse_map,
):
    line, order = plan.line, plan.order
    coarse = coarse_rows[0, 0]
    rows = jnp.transpose(interface_rows, (0, 2, 1, 3))[0]
    whole = pl.BlockSpec(memory_space=pltpu.VMEM)
    outside = pl.BlockSpec(memory_space=pltpu.HBM)
    params = pltpu.CompilerParams(vmem_limit_bytes=VMEM_BYTES)

    def shape(*dims, kind=F32):
        return jax.ShapeDtypeStruct(dims, kind)

    def swap(value, axis, distance):
        size = lax.axis_size(axis)
        return lax.ppermute(value, axis, [(at, at ^ distance) for at in range(size)])

    def line_blocks(messages, riders=()):
        blocks = [messages[0]] + [None] * (line - 1)
        carried = []
        for far in reversed(range(2, line, 2)):
            blocks[far] = swap(messages[far // 2], "sub", far)
        blocks[1] = swap(messages[0], "sub", 1)
        for far in reversed(range(2, line, 2)):
            blocks[far + 1] = swap(blocks[far], "sub", 1)
        for rider, distance in riders:
            rider = lax.optimization_barrier([rider] + [blocks[k] for k in (1,)])[0]
            carried.append(swap(rider, "grp", distance))
        return blocks, carried

    lists = (neighbors[0], rows, coarse_map[0])
    kept = (dirichlet_schur[0, 0], subdomain_loads[0, 0], coupling[0, 0].T, flexibility[0, 0])
    inputs = [pltpu.with_memory_space_constraint(array, pltpu.HBM) for array in lists + kept]
    message, place, weight, schur_place, schur, loads, coupling_t, flex = pl.pallas_call(
        functools.partial(prepare_kernel, plan),
        out_shape=(
            shape(plan.first, 128, kind=BF16),
            shape(order, plan.wide, kind=BF16),
            shape(order, 128, kind=BF16),
            shape(order, plan.wide, kind=BF16),
        )
        + tuple(shape(*array.shape, kind=BF16) for array in kept),
        in_specs=[outside] * 7,
        out_specs=(whole,) * 8,
        scratch_shapes=[pltpu.VMEM(array.shape, array.dtype) for array in lists]
        + [
            pltpu.VMEM((round_up(plan.neighbors, 8), plan.wide), jnp.int32),
            pltpu.VMEM((8, 128), F32),
            pltpu.SemaphoreType.DMA((7,)),
        ],
        compiler_params=params,
        name="prepare",
    )(*inputs)
    riders = [(coarse, distance) for distance in reversed(range(1, plan.groups))]
    first, carried = line_blocks([message] * (line // 2), riders)
    coarse_all = [coarse] + carried[::-1]

    message, image, direction, local_part, far_image, schur_rows, missing = pl.pallas_call(
        functools.partial(direction_kernel, plan),
        out_shape=(
            shape(plan.second, 128, kind=BF16),
            shape(order, 128),
            shape(order, 128),
            shape(order, 128),
            shape(plan.wide, 128),
            shape(plan.each * (line - 1), 128, kind=BF16),
            shape(line, 128),
        ),
        in_specs=[whole] * (line + plan.groups + 5),
        out_specs=(whole,) * 7,
        scratch_shapes=[
            pltpu.VMEM((line, plan.wide, 128), BF16),
            pltpu.VMEM((line, plan.pairs, 128), F32),
            pltpu.VMEM((line, plan.wide, 128), F32),
            pltpu.VMEM((line, plan.spread, 128), F32),
            pltpu.VMEM((line, plan.pairs + plan.half, 128), BF16),
        ],
        compiler_params=params,
        name="direction",
    )(*first, *coarse_all, schur, flex, loads, place, weight)
    heard = [message]
    for step in range(1, plan.groups):
        heard.append(swap(message, "grp", step))

    surface_image, *messages = pl.pallas_call(
        functools.partial(surface_kernel, plan),
        out_shape=(shape(order, 128),)
        + (shape(plan.third, 128, kind=BF16),) * (line // 2),
        in_specs=[whole] * (plan.groups + 6),
        out_specs=(whole,) * (1 + line // 2),
        compiler_params=params,
        name="surface",
    )(*heard, missing, schur, coupling_t, place, weight, local_part)
    last, _ = line_blocks(messages)

    solved, preconditioned = pl.pallas_call(
        functools.partial(result_kernel, plan),
        out_shape=(shape(order, 128), shape(order, 128)),
        in_specs=[whole] * (line + 9),
        out_specs=(outside, outside),
        scratch_shapes=[
            pltpu.VMEM((line, plan.wide, 128), BF16),
            pltpu.VMEM((plan.wide, 128), F32),
            pltpu.VMEM((order, 128), F32),
            pltpu.VMEM((order, 128), F32),
            pltpu.SemaphoreType.DMA((2,)),
        ],
        compiler_params=params,
        name="result",
    )(*last, schur_rows, missing, far_image, image, direction, surface_image, schur_place, place, weight)
    return solved[None, None], preconditioned[None, None]


def wide_body(
    flexibility,
    dirichlet_schur,
    subdomain_loads,
    coupling,
    coarse_rows,
    neighbors,
    interface_rows,
    coarse_map,
):
    flex_block = flexibility[0, 0]
    schur_block = dirichlet_schur[0, 0]
    loads_block = subdomain_loads[0, 0]
    couple_block = coupling[0, 0]
    coarse_block = coarse_rows[0, 0]
    neighbor_ids = neighbors[0, 0]
    row_lists = interface_rows[0, 0]
    corner_ids = coarse_map[0, 0]
    order_size = flex_block.shape[0]
    column_count = loads_block.shape[1]
    coarse_size = coarse_block.shape[1]
    line_size = lax.axis_size("sub")
    flat_rows = row_lists.reshape(-1)
    destinations = (
        jnp.arange(line_size, dtype=jnp.int32)[:, None] == neighbor_ids[None, :]
    ).astype(jnp.bfloat16)
    pair_mask = jnp.zeros((order_size,), jnp.float32).at[flat_rows].set(1.0)
    weight = (1.0 - 0.5 * pair_mask)[:, None]

    def jump_field(surface):
        picked = surface[flat_rows].reshape(row_lists.shape + (column_count,))
        outgoing = jnp.einsum(
            "dk,kjc->djc", destinations, picked, preferred_element_type=jnp.float32
        ).astype(jnp.bfloat16)
        incoming = lax.all_to_all(outgoing, "sub", split_axis=0, concat_axis=0, tiled=True)
        matched = jnp.einsum(
            "dk,djc->kjc", destinations, incoming, preferred_element_type=jnp.float32
        )
        placed = (
            jnp.zeros((order_size, column_count), jnp.float32)
            .at[flat_rows]
            .set(matched.reshape(-1, column_count))
        )
        return surface.astype(jnp.float32) - placed

    def precondition(residual):
        scaled = (weight * residual).astype(jnp.bfloat16)
        schur_image = jnp.dot(schur_block, scaled, preferred_element_type=jnp.float32).astype(
            jnp.bfloat16
        )
        return weight * jump_field(schur_image)

    def column_dot(first_field, second_field):
        return lax.psum(jnp.sum(weight * first_field * second_field, axis=0), ("sub", "grp"))

    residual = jump_field(loads_block)
    zfield = precondition(residual)
    direction = zfield
    inner = column_dot(residual, zfield)
    dir_half = direction.astype(jnp.bfloat16)
    local_part = jnp.dot(flex_block, dir_half, preferred_element_type=jnp.float32)
    coarse_in = jnp.dot(couple_block.T, dir_half, preferred_element_type=jnp.float32)
    dense_sum = jnp.zeros((coarse_size, column_count), jnp.float32).at[corner_ids].set(coarse_in)
    partial_rows = lax.psum_scatter(dense_sum, "grp", scatter_dimension=0, tiled=True)
    panel_half = lax.psum(partial_rows, "sub").astype(jnp.bfloat16)
    coarse_val = jnp.dot(
        coarse_block,
        lax.all_gather(panel_half, "grp", axis=0, tiled=True),
        preferred_element_type=jnp.float32,
    ).astype(jnp.bfloat16)
    surface = (
        local_part + jnp.dot(couple_block, coarse_val, preferred_element_type=jnp.float32)
    ).astype(jnp.bfloat16)
    operated = jump_field(surface)
    step_size = inner / column_dot(direction, operated)
    solution = step_size * direction
    residual = residual - step_size * operated
    zfield = precondition(residual)
    return (solution[None, None], zfield[None, None])


def body(*arrays):
    flexibility, _, loads, _, coarse_rows, neighbors, interface_rows, _ = arrays
    plan = Plan(
        line=lax.axis_size("sub"),
        groups=lax.axis_size("grp"),
        order=flexibility.shape[2],
        columns=loads.shape[3],
        corners=coarse_rows.shape[2],
        coarse=coarse_rows.shape[3],
        neighbors=neighbors.shape[2],
        each=interface_rows.shape[3],
    )
    if plan.served():
        return line_body(plan, *arrays)
    return wide_body(*arrays)


def solution(mesh):
    placed = (
        P("sub", "grp", None, None),
        P("sub", "grp", None, None),
        P("sub", "grp", None, None),
        P("sub", "grp", None, None),
        P("sub", "grp", None, None),
        P("sub", "grp", None),
        P("sub", "grp", None, None),
        P("sub", "grp", None),
    )
    return jax.shard_map(
        body,
        mesh=mesh,
        in_specs=placed,
        out_specs=(P("sub", "grp", None, None), P("sub", "grp", None, None)),
        check_vma=False,
    )
```

```python
import functools

import jax
import jax.numpy as jnp
from jax import lax
from jax.experimental import pallas as pl
from jax.experimental.pallas import tpu as pltpu
from jax.sharding import PartitionSpec as P

F32 = jnp.float32
BF16 = jnp.bfloat16
VMEM_BYTES = 24 * 1024 * 1024


def round_up(value, unit):
    return -(-value // unit) * unit


class Plan:
    def __init__(self, line, groups, order, columns, corners, coarse, neighbors, each):
        self.line, self.groups = line, groups
        self.order, self.columns = order, columns
        self.corners, self.coarse = corners, coarse
        self.neighbors, self.each = neighbors, each
        self.last = line - 1
        self.pairs = neighbors * each
        self.wide = round_up(self.pairs, 128)
        self.half = self.pairs // 2
        self.spare = 128 - self.pairs
        self.map_lane = self.pairs + self.half - self.spare
        self.image_at = self.pairs
        self.schur_at = 2 * self.pairs
        self.edge_at = self.schur_at + self.half
        self.coarse_at = self.edge_at + self.half
        self.first = self.coarse_at + corners
        self.input_at = groups * corners
        self.dots_at = self.input_at + corners
        self.second = round_up(self.dots_at + 8, 16)
        self.sums_at = self.pairs + 2 * each
        self.third = self.sums_at + 16
        self.spread = round_up(corners, 32)

    def served(self):
        return (
            self.line >= 4
            and self.line & (self.line - 1) == 0
            and self.groups & (self.groups - 1) == 0
            and self.neighbors == self.line - 2
            and self.each % 16 == 0
            and self.columns == 128
            and self.wide == 128
            and self.pairs % 32 == 0
            and self.spare <= self.half < 2 * self.spare
            and 2 * self.corners == self.half
            and self.corners <= 2 * (128 - self.map_lane)
            and self.corners % 8 == 0
            and 128 % self.spread == 0
            and (self.line * self.spread) % 128 == 0
            and self.order % 128 == 0
            and self.coarse % 128 == 0
            and self.coarse <= 128 * 256
        )

    def slots(self):
        return range(self.neighbors)

    def rows(self, slot):
        return slice(self.each * slot, self.each * (slot + 1))


def dot(a, b):
    return jnp.dot(a, b, preferred_element_type=F32)


def dot_over_rows(a, b):
    return lax.dot_general(a, b, (((0,), (0,)), ((), ())), preferred_element_type=F32)


def dot_over_lanes(a, b):
    return lax.dot_general(a, b, (((1,), (1,)), ((), ())), preferred_element_type=F32)


def split(value):
    high = value.astype(BF16).astype(F32)
    return high, value - high


def stack_rows(values, height):
    row = lax.broadcasted_iota(jnp.int32, (height, 128), 0)
    stacked = jnp.zeros((height, 128), F32)
    for at, value in enumerate(values):
        stacked = jnp.where(row == at, value, stacked)
    return stacked


def whole_weight(place):
    ones = jnp.ones((place.shape[1], 128), BF16)
    return 1.0 - 0.5 * dot(place, ones)


def extra_rows(plan, values, missing):
    room = 128 - plan.map_lane
    lane = lax.broadcasted_iota(jnp.int32, (8, 128), 1)
    near = pltpu.roll(values, plan.map_lane, 1)
    far = pltpu.roll(values, plan.map_lane - room, 1)
    rows = [near[0:1], far[0:1], near[1:2], far[1:2], jnp.broadcast_to(missing, (1, 128))]
    return jnp.where(lane >= plan.map_lane, stack_rows(rows, 8), 0.0)


def map_rows(plan, extra):
    room = 128 - plan.map_lane
    lane = lax.broadcasted_iota(jnp.int32, (1, 128), 1)
    near = pltpu.roll(extra, room, 1)
    far = pltpu.roll(extra, 2 * room, 1)
    return [jnp.where(lane < room, near[at : at + 1], far[at + 1 : at + 2]) for at in (0, 2)]


def missing_of(plan, extra):
    return jnp.broadcast_to(extra[4:5, plan.map_lane : plan.map_lane + 1], (plan.each, 128))


def last_block(plan, missing, blocks):
    found = jnp.zeros((plan.each, 128), F32)
    for slot in plan.slots():
        found = jnp.where(missing == slot + 1.0, blocks(slot), found)
    return found


def gather_pairs(plan, t, missing, blocks, store):
    far = t ^ plan.last
    last = last_block(plan, missing[far], functools.partial(blocks, far))
    for slot in plan.slots():
        value = blocks(t ^ (slot + 1), slot)
        store(slot, jnp.where(missing[t] == slot + 1.0, last, value))


def prepare_kernel(
    plan,
    neighbors_in,
    rows_in,
    corner_map_in,
    schur_in,
    loads_in,
    coupling_in,
    flexibility_in,
    message,
    place,
    weight_out,
    pairs_out,
    image_out,
    schur,
    loads,
    coupling_t,
    flexibility,
    neighbors,
    rows,
    corner_map,
    rows_pad,
    map_pad,
    arrived,
):
    me = lax.axis_index("sub")
    each, pairs, wide, corners = plan.each, plan.pairs, plan.wide, plan.corners
    sources = (neighbors_in, rows_in, corner_map_in, loads_in, coupling_in, schur_in)
    targets = (neighbors, rows, corner_map, loads, coupling_t, schur)
    sources += (flexibility_in,)
    targets += (flexibility,)
    copies = [
        pltpu.make_async_copy(source, target, arrived.at[at])
        for at, (source, target) in enumerate(zip(sources, targets))
    ]
    for copy in copies:
        copy.start()
    rows_pad[...] = jnp.zeros(rows_pad.shape, jnp.int32)
    map_pad[...] = jnp.zeros(map_pad.shape, F32)
    copies[0].wait()
    copies[1].wait()
    for k in range(plan.neighbors):
        rows_pad[k : k + 1, 0:each] = rows[k]
    spread = rows_pad[...]
    reach = each
    while reach < wide:
        spread = spread + pltpu.roll(spread, reach, 1)
        reach *= 2
    lane = lax.broadcasted_iota(jnp.int32, (1, wide), 1)
    distances = neighbors[...] ^ me
    missing = jnp.full((1, 1), plan.line * (plan.line - 1) // 2, jnp.int32)
    for k in range(plan.neighbors):
        missing = missing - distances[0:1, k : k + 1]
    index = jnp.full((1, wide), -1, jnp.int32)
    for k in range(plan.neighbors):
        distance = distances[0:1, k : k + 1]
        home = jnp.where(distance == plan.last, missing, distance)
        index = jnp.where(lane // each + 1 == home, spread[k : k + 1], index)
    wide_index = jnp.broadcast_to(index.astype(F32), (wide, wide))
    tall_index = wide_index.T.astype(jnp.int32)
    order_rows = lax.broadcasted_iota(jnp.int32, (plan.order, wide), 0)
    place_v = jnp.where(order_rows == index, 1.0, 0.0).astype(BF16)
    place[...] = place_v
    order_lanes = lax.broadcasted_iota(jnp.int32, (wide, plan.order), 1)
    pick_f = jnp.where(order_lanes == tall_index[:, 0:1], 1.0, 0.0)
    weight_row = 1.0 - 0.5 * jnp.sum(pick_f, axis=0, keepdims=True)
    pick = pick_f.astype(BF16)[:pairs]
    weight = whole_weight(place_v)
    weight_out[...] = weight.astype(BF16)
    copies[2].wait()
    corner_ids = corner_map[...]
    map_pad[0:1, 0:corners] = (corner_ids // 128).astype(F32)
    map_pad[1:2, 0:corners] = (corner_ids % 128).astype(F32)
    extra = extra_rows(plan, map_pad[...], missing.astype(F32))
    copies[3].wait()
    load = loads[...]
    weighted = (weight * load.astype(F32)).astype(BF16)
    message[0:pairs, :] = dot(pick, load).astype(BF16)
    copies[4].wait()
    couple = coupling_t[...]
    couple_w = couple.astype(F32) * weight_row
    edge = dot(couple, place_v)
    copies[5].wait()
    image = dot(schur[...], jnp.concatenate([weighted, place_v], axis=1))
    pairs_out[:, :128] = (weight * (0.5 * image[:, 128:])).astype(BF16)
    pairs_out[:, 128:] = (weight * place_v.astype(F32)).astype(BF16)
    image_out[...] = weight * image[:, :128]
    image = image.astype(BF16)
    picks = jnp.concatenate([pick_f[:pairs], couple_w], axis=0).astype(BF16)
    first = dot(picks, image)
    first, first_c = first[:pairs], first[pairs:]
    half, spare = plan.half, plan.spare
    lane = lax.broadcasted_iota(jnp.int32, (half, 128), 1)
    block = 0.5 * first[:, 128:]
    upper, quarter = block[:half], block[half:]
    upper = jnp.where(lane < pairs, upper, pltpu.roll(quarter, pairs - half, 1))
    coarse_part = 0.5 * jnp.concatenate([first_c[:, 128:], edge], axis=0)
    rest = jnp.where(lane < plan.map_lane, pltpu.roll(quarter, pairs - half - spare, 1), 0.0)
    coarse_part = jnp.where(lane < pairs, coarse_part, rest)
    coarse_part = jnp.concatenate([coarse_part[:8] + extra, coarse_part[8:]], axis=0)
    message[plan.image_at : plan.image_at + pairs, :] = first[:, :128].astype(BF16)
    message[plan.schur_at : plan.edge_at, :] = upper.astype(BF16)
    message[plan.edge_at : plan.coarse_at, :] = coarse_part.astype(BF16)
    message[plan.coarse_at :, :] = first_c[:, :128].astype(BF16)
    copies[6].wait()


def direction_kernel(plan, *refs):
    line, pairs, corners = plan.line, plan.pairs, plan.corners
    received, refs = refs[:line], refs[line:]
    coarse_refs, refs = refs[: plan.groups], refs[plan.groups :]
    loads, place, weight, pair_fields, image, flexibility = refs[:6]
    message, direction, local_part, schur_rows, missing_out = refs[6:11]
    moved, images, moved_images, inputs, products = refs[11:]
    half, spare = plan.half, plan.spare
    extras = [block[plan.edge_at : plan.edge_at + 16, :].astype(F32) for block in received]
    missing = [missing_of(plan, extra) for extra in extras]
    missing_out[...] = stack_rows([value[0:1] for value in missing], line)
    codes = []
    per_tile = 128 // plan.spread
    lane = lax.broadcasted_iota(jnp.int32, (1, 128), 1)
    for first in range(0, line, per_tile):
        code = jnp.full((1, 128), -1, jnp.int32)
        for u in range(first, first + per_tile):
            high, low = map_rows(plan, extras[u][:8])
            number = (128.0 * high + low).astype(jnp.int32)
            number = jnp.where(lane < corners, number, -1)
            code = jnp.maximum(code, pltpu.roll(number, (u - first) * plan.spread, 1))
        codes.append(code)
    codes = jnp.concatenate(codes, axis=1)
    coarse_rows = lax.broadcasted_iota(jnp.int32, (plan.coarse, codes.shape[1]), 0)
    chooser = jnp.where(coarse_rows == codes, 1.0, 0.0).astype(BF16)
    coarse_all = jnp.concatenate([ref[...] for ref in coarse_refs], axis=0)
    coarse_matrix = dot(coarse_all, chooser).astype(BF16)

    def loads_block(d, slot):
        return received[d][plan.rows(slot), :].astype(F32)

    def image_block(d, slot):
        return images[d, plan.rows(slot), :]

    changes = []
    for t in range(line):

        def store_loads(slot, value, t=t):
            moved[t, plan.rows(slot), :] = value.astype(BF16)

        gather_pairs(plan, t, missing, loads_block, store_loads)
        if plan.wide > pairs:
            moved[t, pairs:, :] = jnp.zeros((plan.wide - pairs, 128), BF16)
        upper = received[t][plan.schur_at : plan.edge_at, :]
        coarse_part = received[t][plan.edge_at : plan.coarse_at, :]
        upper_f, coarse_f = upper.astype(F32), coarse_part.astype(F32)
        blank = jnp.zeros((128 - half, 128), F32)
        turned = jnp.concatenate([upper_f, blank], axis=0).T[half:pairs]
        near = pltpu.roll(upper_f, 128 - pairs + half, 1)
        far = pltpu.roll(coarse_f, 128 - pairs + half + spare, 1)
        lower = jnp.where(lane < half + spare, near, far)
        lower = jnp.where(lane < half, turned, jnp.where(lane < pairs, lower, 0.0))
        products[t, 0:half, :] = upper
        products[t, half:pairs, :] = lower.astype(BF16)
        products[t, pairs:, :] = coarse_part
        result = dot(products[t], moved[t])
        pair_image = received[t][plan.image_at : plan.schur_at, :].astype(F32)
        images[t] = pair_image - result[:pairs]
        changes.append(result[pairs : pairs + corners])
    for t in range(line):

        def store_image(slot, value, t=t):
            moved_images[t, plan.rows(slot), :] = value

        gather_pairs(plan, t, missing, image_block, store_image)
        if plan.wide > pairs:
            moved_images[t, pairs:, :] = jnp.zeros((plan.wide - pairs, 128), F32)
        edge = dot(products[t, pairs:, :], moved_images[t].astype(BF16))
        coarse_part = received[t][plan.coarse_at :, :].astype(F32)
        entry = coarse_part - changes[t] - edge[corners:]
        parts = [entry]
        if plan.spread > corners:
            parts.append(jnp.zeros((plan.spread - corners, 128), F32))
        inputs[t] = jnp.concatenate(parts, axis=0)
    coarse_in = inputs[...].reshape(line * plan.spread, 128).astype(BF16)
    coarse_out = dot(coarse_matrix, coarse_in)

    for t in range(1, line):
        if t < plan.last:
            rows = products[t, plan.rows(t - 1), :]
        else:
            rows = last_block(
                plan, missing[t], lambda slot: products[plan.last, plan.rows(slot), :].astype(F32)
            ).astype(BF16)
        schur_rows[plan.rows(t - 1), :] = rows
    weight = weight[...].astype(F32)
    right = loads[...].astype(F32) - dot(place[...], moved[0])
    heard = jnp.concatenate([moved[0], moved_images[0].astype(BF16)], axis=0)
    field = image[...] - dot(pair_fields[...], heard)
    local = dot(flexibility[...], field.astype(BF16))
    direction[...] = field
    local_part[...] = local
    inner = split(jnp.sum(weight * right * field, axis=0, keepdims=True))
    square = split(jnp.sum(field * local, axis=0, keepdims=True))
    parts = [coarse_out, inputs[0][:corners], stack_rows(inner + square, 8)]
    if plan.second > plan.dots_at + 8:
        parts.append(jnp.zeros((plan.second - plan.dots_at - 8, 128), F32))
    message[...] = jnp.concatenate(parts, axis=0).astype(BF16)


def local_kernel(plan, local_part, schur, place, weight, pair_rows):
    local = local_part[...]
    high, low = split(local)
    image = dot(schur[...], (weight[...].astype(F32) * local).astype(BF16))
    values = jnp.concatenate([high, low, image], axis=1).astype(BF16)
    rows = dot_over_rows(place[...], values)[: plan.pairs]
    pair_rows[:, :128] = rows[:, :128] + rows[:, 128:256]
    pair_rows[:, 128:] = rows[:, 256:]


def coarse_kernel(plan, *refs):
    groups, corners, pairs = plan.groups, plan.corners, plan.pairs
    heard = [ref[...].astype(F32) for ref in refs[:groups]]
    missing_rows, first, pair_rows = refs[groups : groups + 3]
    own_out, messages = refs[groups + 3], refs[groups + 4 :]
    dots = sum(block[plan.dots_at : plan.dots_at + 8] for block in heard)
    inner = dots[0:1] + dots[1:2]
    square = dots[2:3] + dots[3:4]
    own = None
    for m in range(groups):
        value = 0.0
        for d in range(groups):
            at = corners * (m ^ d)
            value = value + heard[d][at : at + corners]
        value = value.astype(BF16).astype(F32)
        if m == 0:
            own = value
        entry = heard[m][plan.input_at : plan.input_at + corners]
        square = square + jnp.sum(entry * value, axis=0, keepdims=True)
    own_out[...] = own
    twice, blank = 2.0 * own, jnp.zeros((corners, 128), F32)
    values = jnp.concatenate(
        [jnp.concatenate([blank, twice], axis=1), jnp.concatenate([twice, blank], axis=1)], axis=0
    ).astype(BF16)
    coupled = first[plan.edge_at : plan.coarse_at, :]
    both = pair_rows[...] + dot_over_rows(coupled, values)[:pairs]
    surface_part = both[:, :128].astype(BF16)
    sums = stack_rows(split(inner) + split(square), 16).astype(BF16)
    missing = jnp.broadcast_to(missing_rows[0:1, :], (plan.each, 128))

    def image_part(distance):
        if distance == 0:
            return jnp.zeros((plan.each, 128), F32)
        if distance == plan.last:
            return last_block(plan, missing, lambda slot: image_part(slot + 1))
        return both[plan.rows(distance - 1), 128:]

    for far, message in zip(range(0, plan.line, 2), messages):
        message[0:pairs, :] = surface_part
        message[pairs : pairs + plan.each, :] = image_part(far).astype(BF16)
        message[pairs + plan.each : plan.sums_at, :] = image_part(far + 1).astype(BF16)
        message[plan.sums_at :, :] = sums


def surface_kernel(plan, own, schur, coupling_t, weight, local_part, image_out):
    lifted = dot_over_rows(coupling_t[...], own[...].astype(BF16))
    field = (local_part[...] + lifted).astype(BF16)
    scaled = (weight[...].astype(F32) * field.astype(F32)).astype(BF16)
    image_out[...] = weight[...].astype(F32) * dot(schur[...], scaled)


def result_kernel(plan, *refs):
    line, pairs, each = plan.line, plan.pairs, plan.each
    received, schur_rows, missing_rows, refs = refs[:line], refs[line], refs[line + 1], refs[line + 2 :]
    direction, surface_image, pair_fields = refs[:3]
    solution_out, preconditioned_out = refs[3:5]
    moved, far_rows, solved, preconditioned, sent = refs[5:]
    sums = 0.0
    for block in received:
        sums = sums + block[plan.sums_at :, :].astype(F32)
    step = (sums[0:1] + sums[1:2]) / (sums[2:3] + sums[3:4])
    solved[...] = step * direction[...]
    solution_copy = pltpu.make_async_copy(solved, solution_out, sent.at[0])
    solution_copy.start()
    missing = [jnp.broadcast_to(missing_rows[t : t + 1, :], (each, 128)) for t in range(line)]

    def surface_block(d, slot):
        return received[d][plan.rows(slot), :].astype(F32)

    changes = []
    for t in range(line):

        def store_surface(slot, value, t=t):
            moved[t, plan.rows(slot), :] = value.astype(BF16)

        gather_pairs(plan, t, missing, surface_block, store_surface)
        if plan.wide > pairs:
            moved[t, pairs:, :] = jnp.zeros((plan.wide - pairs, 128), BF16)
        if t == 0:
            continue

        block = schur_rows[plan.rows(t - 1), :]
        at = pairs + each * (t % 2)
        image = received[t][at : at + each, :].astype(F32)
        changes.append(image - dot(block, moved[t]))
    for slot in plan.slots():
        far_rows[plan.rows(slot), :] = jnp.where(
            missing[0] == slot + 1.0, changes[plan.last - 1], changes[slot]
        )
    if plan.wide > pairs:
        far_rows[pairs:, :] = jnp.zeros((plan.wide - pairs, 128), F32)
    heard = jnp.concatenate([moved[0], far_rows[...].astype(BF16)], axis=0)
    change = surface_image[...] - dot(pair_fields[...], heard)
    preconditioned[...] = direction[...] - step * change
    last_copy = pltpu.make_async_copy(preconditioned, preconditioned_out, sent.at[1])
    last_copy.start()
    solution_copy.wait()
    last_copy.wait()


def line_body(
    plan,
    flexibility,
    dirichlet_schur,
    subdomain_loads,
    coupling,
    coarse_rows,
    neighbors,
    interface_rows,
    coarse_map,
):
    line, order = plan.line, plan.order
    coarse = coarse_rows[0, 0]
    rows = jnp.transpose(interface_rows, (0, 2, 1, 3))[0]
    whole = pl.BlockSpec(memory_space=pltpu.VMEM)
    outside = pl.BlockSpec(memory_space=pltpu.HBM)
    params = pltpu.CompilerParams(vmem_limit_bytes=VMEM_BYTES)

    def shape(*dims, kind=F32):
        return jax.ShapeDtypeStruct(dims, kind)

    def swap(value, axis, distance):
        size = lax.axis_size(axis)
        return lax.ppermute(value, axis, [(at, at ^ distance) for at in range(size)])

    def line_blocks(messages, riders=()):
        blocks = [messages[0]] + [None] * (line - 1)
        carried = []
        for far in reversed(range(2, line, 2)):
            blocks[far] = swap(messages[far // 2], "sub", far)
        blocks[1] = swap(messages[0], "sub", 1)
        for far in reversed(range(2, line, 2)):
            blocks[far + 1] = swap(blocks[far], "sub", 1)
        for rider, distance in riders:
            rider = lax.optimization_barrier([rider] + [blocks[k] for k in (1,)])[0]
            carried.append(swap(rider, "grp", distance))
        return blocks, carried

    lists = (neighbors[0], rows, coarse_map[0])
    kept = (dirichlet_schur[0, 0], subdomain_loads[0, 0], coupling[0, 0].T, flexibility[0, 0])
    inputs = [pltpu.with_memory_space_constraint(array, pltpu.HBM) for array in lists + kept]
    message, place, weight, pair_fields, image, schur, loads, coupling_t, flex = pl.pallas_call(
        functools.partial(prepare_kernel, plan),
        out_shape=(
            shape(plan.first, 128, kind=BF16),
            shape(order, plan.wide, kind=BF16),
            shape(order, 128, kind=BF16),
            shape(order, 2 * plan.wide, kind=BF16),
            shape(order, 128),
        )
        + tuple(shape(*array.shape, kind=BF16) for array in kept),
        in_specs=[outside] * 7,
        out_specs=(whole,) * 9,
        scratch_shapes=[pltpu.VMEM(array.shape, array.dtype) for array in lists]
        + [
            pltpu.VMEM((round_up(plan.neighbors, 8), plan.wide), jnp.int32),
            pltpu.VMEM((8, 128), F32),
            pltpu.SemaphoreType.DMA((7,)),
        ],
        compiler_params=params,
        name="prepare",
    )(*inputs)
    riders = [(coarse, distance) for distance in reversed(range(1, plan.groups))]
    first, carried = line_blocks([message] * (line // 2), riders)
    coarse_all = [coarse] + carried[::-1]

    message, direction, local_part, schur_rows, missing = pl.pallas_call(
        functools.partial(direction_kernel, plan),
        out_shape=(
            shape(plan.second, 128, kind=BF16),
            shape(order, 128),
            shape(order, 128),
            shape(plan.each * (line - 1), 128, kind=BF16),
            shape(line, 128),
        ),
        in_specs=[whole] * (line + plan.groups + 6),
        out_specs=(whole,) * 5,
        scratch_shapes=[
            pltpu.VMEM((line, plan.wide, 128), BF16),
            pltpu.VMEM((line, plan.pairs, 128), F32),
            pltpu.VMEM((line, plan.wide, 128), F32),
            pltpu.VMEM((line, plan.spread, 128), F32),
            pltpu.VMEM((line, plan.pairs + plan.half, 128), BF16),
        ],
        compiler_params=params,
        name="direction",
    )(*first, *coarse_all, loads, place, weight, pair_fields, image, flex)
    heard = [message]
    for step in range(1, plan.groups):
        heard.append(swap(message, "grp", step))

    pair_rows = pl.pallas_call(
        functools.partial(local_kernel, plan),
        out_shape=shape(plan.pairs, 256),
        in_specs=[whole] * 4,
        out_specs=whole,
        compiler_params=params,
        name="local",
    )(local_part, schur, place, weight)
    own, *messages = pl.pallas_call(
        functools.partial(coarse_kernel, plan),
        out_shape=(shape(plan.corners, 128),)
        + (shape(plan.third, 128, kind=BF16),) * (line // 2),
        in_specs=[whole] * (plan.groups + 3),
        out_specs=(whole,) * (1 + line // 2),
        compiler_params=params,
        name="coarse",
    )(*heard, missing, first[0], pair_rows)
    last, _ = line_blocks(messages)
    surface_image = pl.pallas_call(
        functools.partial(surface_kernel, plan),
        out_shape=shape(order, 128),
        in_specs=[whole] * 5,
        out_specs=whole,
        compiler_params=params,
        name="surface",
    )(own, schur, coupling_t, weight, local_part)

    solved, preconditioned = pl.pallas_call(
        functools.partial(result_kernel, plan),
        out_shape=(shape(order, 128), shape(order, 128)),
        in_specs=[whole] * (line + 5),
        out_specs=(outside, outside),
        scratch_shapes=[
            pltpu.VMEM((line, plan.wide, 128), BF16),
            pltpu.VMEM((plan.wide, 128), F32),
            pltpu.VMEM((order, 128), F32),
            pltpu.VMEM((order, 128), F32),
            pltpu.SemaphoreType.DMA((2,)),
        ],
        compiler_params=params,
        name="result",
    )(*last, schur_rows, missing, direction, surface_image, pair_fields)
    return solved[None, None], preconditioned[None, None]


def wide_body(
    flexibility,
    dirichlet_schur,
    subdomain_loads,
    coupling,
    coarse_rows,
    neighbors,
    interface_rows,
    coarse_map,
):
    flex_block = flexibility[0, 0]
    schur_block = dirichlet_schur[0, 0]
    loads_block = subdomain_loads[0, 0]
    couple_block = coupling[0, 0]
    coarse_block = coarse_rows[0, 0]
    neighbor_ids = neighbors[0, 0]
    row_lists = interface_rows[0, 0]
    corner_ids = coarse_map[0, 0]
    order_size = flex_block.shape[0]
    column_count = loads_block.shape[1]
    coarse_size = coarse_block.shape[1]
    line_size = lax.axis_size("sub")
    flat_rows = row_lists.reshape(-1)
    destinations = (
        jnp.arange(line_size, dtype=jnp.int32)[:, None] == neighbor_ids[None, :]
    ).astype(jnp.bfloat16)
    pair_mask = jnp.zeros((order_size,), jnp.float32).at[flat_rows].set(1.0)
    weight = (1.0 - 0.5 * pair_mask)[:, None]

    def jump_field(surface):
        picked = surface[flat_rows].reshape(row_lists.shape + (column_count,))
        outgoing = jnp.einsum(
            "dk,kjc->djc", destinations, picked, preferred_element_type=jnp.float32
        ).astype(jnp.bfloat16)
        incoming = lax.all_to_all(outgoing, "sub", split_axis=0, concat_axis=0, tiled=True)
        matched = jnp.einsum(
            "dk,djc->kjc", destinations, incoming, preferred_element_type=jnp.float32
        )
        placed = (
            jnp.zeros((order_size, column_count), jnp.float32)
            .at[flat_rows]
            .set(matched.reshape(-1, column_count))
        )
        return surface.astype(jnp.float32) - placed

    def precondition(residual):
        scaled = (weight * residual).astype(jnp.bfloat16)
        schur_image = jnp.dot(schur_block, scaled, preferred_element_type=jnp.float32).astype(
            jnp.bfloat16
        )
        return weight * jump_field(schur_image)

    def column_dot(first_field, second_field):
        return lax.psum(jnp.sum(weight * first_field * second_field, axis=0), ("sub", "grp"))

    residual = jump_field(loads_block)
    zfield = precondition(residual)
    direction = zfield
    inner = column_dot(residual, zfield)
    dir_half = direction.astype(jnp.bfloat16)
    local_part = jnp.dot(flex_block, dir_half, preferred_element_type=jnp.float32)
    coarse_in = jnp.dot(couple_block.T, dir_half, preferred_element_type=jnp.float32)
    dense_sum = jnp.zeros((coarse_size, column_count), jnp.float32).at[corner_ids].set(coarse_in)
    partial_rows = lax.psum_scatter(dense_sum, "grp", scatter_dimension=0, tiled=True)
    panel_half = lax.psum(partial_rows, "sub").astype(jnp.bfloat16)
    coarse_val = jnp.dot(
        coarse_block,
        lax.all_gather(panel_half, "grp", axis=0, tiled=True),
        preferred_element_type=jnp.float32,
    ).astype(jnp.bfloat16)
    surface = (
        local_part + jnp.dot(couple_block, coarse_val, preferred_element_type=jnp.float32)
    ).astype(jnp.bfloat16)
    operated = jump_field(surface)
    step_size = inner / column_dot(direction, operated)
    solution = step_size * direction
    residual = residual - step_size * operated
    zfield = precondition(residual)
    return (solution[None, None], zfield[None, None])


def body(*arrays):
    flexibility, _, loads, _, coarse_rows, neighbors, interface_rows, _ = arrays
    plan = Plan(
        line=lax.axis_size("sub"),
        groups=lax.axis_size("grp"),
        order=flexibility.shape[2],
        columns=loads.shape[3],
        corners=coarse_rows.shape[2],
        coarse=coarse_rows.shape[3],
        neighbors=neighbors.shape[2],
        each=interface_rows.shape[3],
    )
    if plan.served():
        return line_body(plan, *arrays)
    return wide_body(*arrays)


def solution(mesh):
    placed = (
        P("sub", "grp", None, None),
        P("sub", "grp", None, None),
        P("sub", "grp", None, None),
        P("sub", "grp", None, None),
        P("sub", "grp", None, None),
        P("sub", "grp", None),
        P("sub", "grp", None, None),
        P("sub", "grp", None),
    )
    return jax.shard_map(
        body,
        mesh=mesh,
        in_specs=placed,
        out_specs=(P("sub", "grp", None, None), P("sub", "grp", None, None)),
        check_vma=False,
    )
```

```python
import functools

import jax
import jax.numpy as jnp
from jax import lax
from jax.experimental import pallas as pl
from jax.experimental.pallas import tpu as pltpu
from jax.sharding import PartitionSpec as P

F32 = jnp.float32
BF16 = jnp.bfloat16
VMEM_BYTES = 24 * 1024 * 1024


def round_up(value, unit):
    return -(-value // unit) * unit


class Plan:
    def __init__(self, line, groups, order, columns, corners, coarse, neighbors, each):
        self.line, self.groups = line, groups
        self.order, self.columns = order, columns
        self.corners, self.coarse = corners, coarse
        self.neighbors, self.each = neighbors, each
        self.last = line - 1
        self.pairs = neighbors * each
        self.wide = round_up(self.pairs, 128)
        self.half = self.pairs // 2
        self.spare = 128 - self.pairs
        self.map_lane = self.pairs + self.half - self.spare
        self.image_at = self.pairs
        self.schur_at = 2 * self.pairs
        self.edge_at = self.schur_at + self.half
        self.coarse_at = self.edge_at + self.half
        self.first = self.coarse_at + corners
        self.input_at = groups * corners
        self.dots_at = self.input_at + corners
        self.second = round_up(self.dots_at + 8, 16)
        self.sums_at = self.pairs + 2 * each
        self.third = self.sums_at + 16
        self.spread = round_up(corners, 32)

    def served(self):
        return (
            self.line >= 4
            and self.line & (self.line - 1) == 0
            and self.groups & (self.groups - 1) == 0
            and self.neighbors == self.line - 2
            and self.each % 16 == 0
            and self.columns == 128
            and self.wide == 128
            and self.pairs % 32 == 0
            and self.spare <= self.half < 2 * self.spare
            and 2 * self.corners == self.half
            and self.corners <= 2 * (128 - self.map_lane)
            and self.corners % 8 == 0
            and 128 % self.spread == 0
            and (self.line * self.spread) % 128 == 0
            and self.order % 128 == 0
            and self.coarse % 128 == 0
            and self.coarse <= 128 * 256
        )

    def slots(self):
        return range(self.neighbors)

    def rows(self, slot):
        return slice(self.each * slot, self.each * (slot + 1))


def dot(a, b):
    return jnp.dot(a, b, preferred_element_type=F32)


def dot_over_rows(a, b):
    return lax.dot_general(a, b, (((0,), (0,)), ((), ())), preferred_element_type=F32)


def dot_over_lanes(a, b):
    return lax.dot_general(a, b, (((1,), (1,)), ((), ())), preferred_element_type=F32)


def split(value):
    high = value.astype(BF16).astype(F32)
    return high, value - high


def stack_rows(values, height):
    row = lax.broadcasted_iota(jnp.int32, (height, 128), 0)
    stacked = jnp.zeros((height, 128), F32)
    for at, value in enumerate(values):
        stacked = jnp.where(row == at, value, stacked)
    return stacked


def whole_weight(place):
    ones = jnp.ones((place.shape[1], 128), BF16)
    return 1.0 - 0.5 * dot(place, ones)


def extra_rows(plan, values, missing):
    room = 128 - plan.map_lane
    lane = lax.broadcasted_iota(jnp.int32, (8, 128), 1)
    near = pltpu.roll(values, plan.map_lane, 1)
    far = pltpu.roll(values, plan.map_lane - room, 1)
    rows = [near[0:1], far[0:1], near[1:2], far[1:2], jnp.broadcast_to(missing, (1, 128))]
    return jnp.where(lane >= plan.map_lane, stack_rows(rows, 8), 0.0)


def map_rows(plan, extra):
    room = 128 - plan.map_lane
    lane = lax.broadcasted_iota(jnp.int32, (1, 128), 1)
    near = pltpu.roll(extra, room, 1)
    far = pltpu.roll(extra, 2 * room, 1)
    return [jnp.where(lane < room, near[at : at + 1], far[at + 1 : at + 2]) for at in (0, 2)]


def missing_of(plan, extra):
    return jnp.broadcast_to(extra[4:5, plan.map_lane : plan.map_lane + 1], (plan.each, 128))


def last_block(plan, missing, blocks):
    found = jnp.zeros((plan.each, 128), F32)
    for slot in plan.slots():
        found = jnp.where(missing == slot + 1.0, blocks(slot), found)
    return found


def gather_pairs(plan, t, missing, blocks, store):
    far = t ^ plan.last
    last = last_block(plan, missing[far], functools.partial(blocks, far))
    for slot in plan.slots():
        value = blocks(t ^ (slot + 1), slot)
        store(slot, jnp.where(missing[t] == slot + 1.0, last, value))


def prepare_kernel(
    plan,
    neighbors_in,
    rows_in,
    corner_map_in,
    schur_in,
    loads_in,
    coupling_in,
    flexibility_in,
    message,
    place,
    weight_out,
    pairs_out,
    image_out,
    schur,
    loads,
    coupling_t,
    flexibility,
    neighbors,
    rows,
    corner_map,
    rows_pad,
    map_pad,
    arrived,
):
    me = lax.axis_index("sub")
    each, pairs, wide, corners = plan.each, plan.pairs, plan.wide, plan.corners
    sources = (neighbors_in, rows_in, corner_map_in, loads_in, coupling_in, schur_in)
    targets = (neighbors, rows, corner_map, loads, coupling_t, schur)
    sources += (flexibility_in,)
    targets += (flexibility,)
    copies = [
        pltpu.make_async_copy(source, target, arrived.at[at])
        for at, (source, target) in enumerate(zip(sources, targets))
    ]
    for copy in copies:
        copy.start()
    rows_pad[...] = jnp.zeros(rows_pad.shape, jnp.int32)
    map_pad[...] = jnp.zeros(map_pad.shape, F32)
    for copy in copies[:3]:
        copy.wait()
    for k in range(plan.neighbors):
        rows_pad[k : k + 1, 0:each] = rows[k]
    spread = rows_pad[...]
    reach = each
    while reach < wide:
        spread = spread + pltpu.roll(spread, reach, 1)
        reach *= 2
    lane = lax.broadcasted_iota(jnp.int32, (1, wide), 1)
    distances = neighbors[...] ^ me
    missing = jnp.full((1, 1), plan.line * (plan.line - 1) // 2, jnp.int32)
    for k in range(plan.neighbors):
        missing = missing - distances[0:1, k : k + 1]
    index = jnp.full((1, wide), -1, jnp.int32)
    for k in range(plan.neighbors):
        distance = distances[0:1, k : k + 1]
        home = jnp.where(distance == plan.last, missing, distance)
        index = jnp.where(lane // each + 1 == home, spread[k : k + 1], index)
    wide_index = jnp.broadcast_to(index.astype(F32), (wide, wide))
    tall_index = wide_index.T.astype(jnp.int32)
    order_rows = lax.broadcasted_iota(jnp.int32, (plan.order, wide), 0)
    place_v = jnp.where(order_rows == index, 1.0, 0.0).astype(BF16)
    place[...] = place_v
    order_lanes = lax.broadcasted_iota(jnp.int32, (wide, plan.order), 1)
    pick_f = jnp.where(order_lanes == tall_index[:, 0:1], 1.0, 0.0)
    weight_row = 1.0 - 0.5 * jnp.sum(pick_f, axis=0, keepdims=True)
    pick = pick_f.astype(BF16)[:pairs]
    weight = whole_weight(place_v)
    weight_out[...] = weight.astype(BF16)
    corner_ids = corner_map[...]
    map_pad[0:1, 0:corners] = (corner_ids // 128).astype(F32)
    map_pad[1:2, 0:corners] = (corner_ids % 128).astype(F32)
    extra = extra_rows(plan, map_pad[...], missing.astype(F32))
    for copy in copies[3:6]:
        copy.wait()
    load = loads[...]
    weighted = (weight * load.astype(F32)).astype(BF16)
    message[0:pairs, :] = dot(pick, load).astype(BF16)
    couple = coupling_t[...]
    couple_w = couple.astype(F32) * weight_row
    image = dot(schur[...], jnp.concatenate([weighted, place_v], axis=1))
    edge = dot(couple, place_v)
    pairs_out[:, :128] = (weight * (0.5 * image[:, 128:])).astype(BF16)
    pairs_out[:, 128:] = (weight * place_v.astype(F32)).astype(BF16)
    image_out[...] = weight * image[:, :128]
    image = image.astype(BF16)
    picks = jnp.concatenate([pick_f[:pairs], couple_w], axis=0).astype(BF16)
    first = dot(picks, image)
    first, first_c = first[:pairs], first[pairs:]
    half, spare = plan.half, plan.spare
    lane = lax.broadcasted_iota(jnp.int32, (half, 128), 1)
    block = 0.5 * first[:, 128:]
    upper, quarter = block[:half], block[half:]
    upper = jnp.where(lane < pairs, upper, pltpu.roll(quarter, pairs - half, 1))
    coarse_part = 0.5 * jnp.concatenate([first_c[:, 128:], edge], axis=0)
    rest = jnp.where(lane < plan.map_lane, pltpu.roll(quarter, pairs - half - spare, 1), 0.0)
    coarse_part = jnp.where(lane < pairs, coarse_part, rest)
    coarse_part = jnp.concatenate([coarse_part[:8] + extra, coarse_part[8:]], axis=0)
    message[plan.image_at : plan.image_at + pairs, :] = first[:, :128].astype(BF16)
    message[plan.schur_at : plan.edge_at, :] = upper.astype(BF16)
    message[plan.edge_at : plan.coarse_at, :] = coarse_part.astype(BF16)
    message[plan.coarse_at :, :] = first_c[:, :128].astype(BF16)
    copies[6].wait()


def direction_kernel(plan, *refs):
    line, pairs, corners = plan.line, plan.pairs, plan.corners
    received, refs = refs[:line], refs[line:]
    coarse_refs, refs = refs[: plan.groups], refs[plan.groups :]
    loads, place, weight, pair_fields, image, flexibility = refs[:6]
    message, direction, local_part, schur_rows, missing_out = refs[6:11]
    moved, images, moved_images, inputs, products = refs[11:]
    half, spare = plan.half, plan.spare
    extras = [block[plan.edge_at : plan.edge_at + 16, :].astype(F32) for block in received]
    missing = [missing_of(plan, extra) for extra in extras]
    missing_out[...] = stack_rows([value[0:1] for value in missing], line)
    codes = []
    per_tile = 128 // plan.spread
    lane = lax.broadcasted_iota(jnp.int32, (1, 128), 1)
    for first in range(0, line, per_tile):
        code = jnp.full((1, 128), -1, jnp.int32)
        for u in range(first, first + per_tile):
            high, low = map_rows(plan, extras[u][:8])
            number = (128.0 * high + low).astype(jnp.int32)
            number = jnp.where(lane < corners, number, -1)
            code = jnp.maximum(code, pltpu.roll(number, (u - first) * plan.spread, 1))
        codes.append(code)
    codes = jnp.concatenate(codes, axis=1)
    coarse_rows = lax.broadcasted_iota(jnp.int32, (plan.coarse, codes.shape[1]), 0)
    chooser = jnp.where(coarse_rows == codes, 1.0, 0.0).astype(BF16)
    coarse_all = jnp.concatenate([ref[...] for ref in coarse_refs], axis=0)
    coarse_matrix = dot(coarse_all, chooser).astype(BF16)

    def loads_block(d, slot):
        return received[d][plan.rows(slot), :].astype(F32)

    def image_block(d, slot):
        return images[d, plan.rows(slot), :]

    changes = []
    for t in range(line):

        def store_loads(slot, value, t=t):
            moved[t, plan.rows(slot), :] = value.astype(BF16)

        gather_pairs(plan, t, missing, loads_block, store_loads)
        if plan.wide > pairs:
            moved[t, pairs:, :] = jnp.zeros((plan.wide - pairs, 128), BF16)
        upper = received[t][plan.schur_at : plan.edge_at, :]
        coarse_part = received[t][plan.edge_at : plan.coarse_at, :]
        upper_f, coarse_f = upper.astype(F32), coarse_part.astype(F32)
        blank = jnp.zeros((128 - half, 128), F32)
        turned = jnp.concatenate([upper_f, blank], axis=0).T[half:pairs]
        near = pltpu.roll(upper_f, 128 - pairs + half, 1)
        far = pltpu.roll(coarse_f, 128 - pairs + half + spare, 1)
        lower = jnp.where(lane < half + spare, near, far)
        lower = jnp.where(lane < half, turned, jnp.where(lane < pairs, lower, 0.0))
        products[t, 0:half, :] = upper
        products[t, half:pairs, :] = lower.astype(BF16)
        products[t, pairs:, :] = coarse_part
        result = dot(products[t], moved[t])
        pair_image = received[t][plan.image_at : plan.schur_at, :].astype(F32)
        images[t] = pair_image - result[:pairs]
        changes.append(result[pairs : pairs + corners])
    for t in range(line):

        def store_image(slot, value, t=t):
            moved_images[t, plan.rows(slot), :] = value

        gather_pairs(plan, t, missing, image_block, store_image)
        if plan.wide > pairs:
            moved_images[t, pairs:, :] = jnp.zeros((plan.wide - pairs, 128), F32)
        edge = dot(products[t, pairs:, :], moved_images[t].astype(BF16))
        coarse_part = received[t][plan.coarse_at :, :].astype(F32)
        entry = coarse_part - changes[t] - edge[corners:]
        parts = [entry]
        if plan.spread > corners:
            parts.append(jnp.zeros((plan.spread - corners, 128), F32))
        inputs[t] = jnp.concatenate(parts, axis=0)
    coarse_in = inputs[...].reshape(line * plan.spread, 128).astype(BF16)
    coarse_out = dot(coarse_matrix, coarse_in)

    for t in range(1, line):
        if t < plan.last:
            rows = products[t, plan.rows(t - 1), :]
        else:
            rows = last_block(
                plan, missing[t], lambda slot: products[plan.last, plan.rows(slot), :].astype(F32)
            ).astype(BF16)
        schur_rows[plan.rows(t - 1), :] = rows
    weight = weight[...].astype(F32)
    right = loads[...].astype(F32) - dot(place[...], moved[0])
    heard = jnp.concatenate([moved[0], moved_images[0].astype(BF16)], axis=0)
    field = image[...] - dot(pair_fields[...], heard)
    local = dot(flexibility[...], field.astype(BF16))
    direction[...] = field
    local_part[...] = local
    inner = split(jnp.sum(weight * right * field, axis=0, keepdims=True))
    square = split(jnp.sum(field * local, axis=0, keepdims=True))
    parts = [coarse_out, inputs[0][:corners], stack_rows(inner + square, 8)]
    if plan.second > plan.dots_at + 8:
        parts.append(jnp.zeros((plan.second - plan.dots_at - 8, 128), F32))
    message[...] = jnp.concatenate(parts, axis=0).astype(BF16)


def local_kernel(plan, local_part, schur, place, weight, pair_rows):
    local = local_part[...]
    high, low = split(local)
    image = dot(schur[...], (weight[...].astype(F32) * local).astype(BF16))
    values = jnp.concatenate([high, low, image], axis=1).astype(BF16)
    rows = dot_over_rows(place[...], values)[: plan.pairs]
    pair_rows[:, :128] = rows[:, :128] + rows[:, 128:256]
    pair_rows[:, 128:] = rows[:, 256:]


def coarse_kernel(plan, *refs):
    groups, corners, pairs = plan.groups, plan.corners, plan.pairs
    heard = [ref[...].astype(F32) for ref in refs[:groups]]
    missing_rows, first, pair_rows = refs[groups : groups + 3]
    own_out, messages = refs[groups + 3], refs[groups + 4 :]
    dots = sum(block[plan.dots_at : plan.dots_at + 8] for block in heard)
    inner = dots[0:1] + dots[1:2]
    square = dots[2:3] + dots[3:4]
    own = None
    for m in range(groups):
        value = 0.0
        for d in range(groups):
            at = corners * (m ^ d)
            value = value + heard[d][at : at + corners]
        value = value.astype(BF16).astype(F32)
        if m == 0:
            own = value
        entry = heard[m][plan.input_at : plan.input_at + corners]
        square = square + jnp.sum(entry * value, axis=0, keepdims=True)
    own_out[...] = own
    twice, blank = 2.0 * own, jnp.zeros((corners, 128), F32)
    values = jnp.concatenate(
        [jnp.concatenate([blank, twice], axis=1), jnp.concatenate([twice, blank], axis=1)], axis=0
    ).astype(BF16)
    coupled = first[plan.edge_at : plan.coarse_at, :]
    both = pair_rows[...] + dot_over_rows(coupled, values)[:pairs]
    surface_part = both[:, :128].astype(BF16)
    sums = stack_rows(split(inner) + split(square), 16).astype(BF16)
    missing = jnp.broadcast_to(missing_rows[0:1, :], (plan.each, 128))

    def image_part(distance):
        if distance == 0:
            return jnp.zeros((plan.each, 128), F32)
        if distance == plan.last:
            return last_block(plan, missing, lambda slot: image_part(slot + 1))
        return both[plan.rows(distance - 1), 128:]

    for far, message in zip(range(0, plan.line, 2), messages):
        message[0:pairs, :] = surface_part
        message[pairs : pairs + plan.each, :] = image_part(far).astype(BF16)
        message[pairs + plan.each : plan.sums_at, :] = image_part(far + 1).astype(BF16)
        message[plan.sums_at :, :] = sums


def surface_kernel(plan, own, schur, coupling_t, weight, local_part, image_out):
    lifted = dot_over_rows(coupling_t[...], own[...].astype(BF16))
    field = (local_part[...] + lifted).astype(BF16)
    scaled = (weight[...].astype(F32) * field.astype(F32)).astype(BF16)
    image_out[...] = weight[...].astype(F32) * dot(schur[...], scaled)


def result_kernel(plan, *refs):
    line, pairs, each = plan.line, plan.pairs, plan.each
    received, schur_rows, missing_rows, refs = refs[:line], refs[line], refs[line + 1], refs[line + 2 :]
    direction, surface_image, pair_fields = refs[:3]
    solution_out, preconditioned_out = refs[3:5]
    moved, far_rows, solved, preconditioned, sent = refs[5:]
    sums = 0.0
    for block in received:
        sums = sums + block[plan.sums_at :, :].astype(F32)
    step = (sums[0:1] + sums[1:2]) / (sums[2:3] + sums[3:4])
    solved[...] = step * direction[...]
    solution_copy = pltpu.make_async_copy(solved, solution_out, sent.at[0])
    solution_copy.start()
    missing = [jnp.broadcast_to(missing_rows[t : t + 1, :], (each, 128)) for t in range(line)]

    def surface_block(d, slot):
        return received[d][plan.rows(slot), :].astype(F32)

    changes = []
    for t in range(line):

        def store_surface(slot, value, t=t):
            moved[t, plan.rows(slot), :] = value.astype(BF16)

        gather_pairs(plan, t, missing, surface_block, store_surface)
        if plan.wide > pairs:
            moved[t, pairs:, :] = jnp.zeros((plan.wide - pairs, 128), BF16)
        if t == 0:
            continue

        block = schur_rows[plan.rows(t - 1), :]
        at = pairs + each * (t % 2)
        image = received[t][at : at + each, :].astype(F32)
        changes.append(image - dot(block, moved[t]))
    for slot in plan.slots():
        far_rows[plan.rows(slot), :] = jnp.where(
            missing[0] == slot + 1.0, changes[plan.last - 1], changes[slot]
        )
    if plan.wide > pairs:
        far_rows[pairs:, :] = jnp.zeros((plan.wide - pairs, 128), F32)
    heard = jnp.concatenate([moved[0], far_rows[...].astype(BF16)], axis=0)
    change = surface_image[...] - dot(pair_fields[...], heard)
    preconditioned[...] = direction[...] - step * change
    last_copy = pltpu.make_async_copy(preconditioned, preconditioned_out, sent.at[1])
    last_copy.start()
    solution_copy.wait()
    last_copy.wait()


def line_body(
    plan,
    flexibility,
    dirichlet_schur,
    subdomain_loads,
    coupling,
    coarse_rows,
    neighbors,
    interface_rows,
    coarse_map,
):
    line, order = plan.line, plan.order
    coarse = coarse_rows[0, 0]
    rows = jnp.transpose(interface_rows, (0, 2, 1, 3))[0]
    whole = pl.BlockSpec(memory_space=pltpu.VMEM)
    outside = pl.BlockSpec(memory_space=pltpu.HBM)
    params = pltpu.CompilerParams(vmem_limit_bytes=VMEM_BYTES)

    def shape(*dims, kind=F32):
        return jax.ShapeDtypeStruct(dims, kind)

    def swap(value, axis, distance):
        size = lax.axis_size(axis)
        return lax.ppermute(value, axis, [(at, at ^ distance) for at in range(size)])

    def line_blocks(messages, riders=()):
        blocks = [messages[0]] + [None] * (line - 1)
        carried = []
        for far in reversed(range(2, line, 2)):
            blocks[far] = swap(messages[far // 2], "sub", far)
        blocks[1] = swap(messages[0], "sub", 1)
        for far in reversed(range(2, line, 2)):
            blocks[far + 1] = swap(blocks[far], "sub", 1)
        for (rider, distance), k in zip(riders, (1, 2, 1)):
            rider = lax.optimization_barrier([rider, blocks[k]])[0]
            carried.append(swap(rider, "grp", distance))
        return blocks, carried

    lists = (neighbors[0], rows, coarse_map[0])
    kept = (dirichlet_schur[0, 0], subdomain_loads[0, 0], coupling[0, 0].T, flexibility[0, 0])
    inputs = [pltpu.with_memory_space_constraint(array, pltpu.HBM) for array in lists + kept]
    message, place, weight, pair_fields, image, schur, loads, coupling_t, flex = pl.pallas_call(
        functools.partial(prepare_kernel, plan),
        out_shape=(
            shape(plan.first, 128, kind=BF16),
            shape(order, plan.wide, kind=BF16),
            shape(order, 128, kind=BF16),
            shape(order, 2 * plan.wide, kind=BF16),
            shape(order, 128),
        )
        + tuple(shape(*array.shape, kind=BF16) for array in kept),
        in_specs=[outside] * 7,
        out_specs=(whole,) * 9,
        scratch_shapes=[pltpu.VMEM(array.shape, array.dtype) for array in lists]
        + [
            pltpu.VMEM((round_up(plan.neighbors, 8), plan.wide), jnp.int32),
            pltpu.VMEM((8, 128), F32),
            pltpu.SemaphoreType.DMA((7,)),
        ],
        compiler_params=params,
        name="prepare",
    )(*inputs)
    riders = [(coarse, distance) for distance in reversed(range(1, plan.groups))]
    first, carried = line_blocks([message] * (line // 2), riders)
    coarse_all = [coarse] + carried[::-1]

    message, direction, local_part, schur_rows, missing = pl.pallas_call(
        functools.partial(direction_kernel, plan),
        out_shape=(
            shape(plan.second, 128, kind=BF16),
            shape(order, 128),
            shape(order, 128),
            shape(plan.each * (line - 1), 128, kind=BF16),
            shape(line, 128),
        ),
        in_specs=[whole] * (line + plan.groups + 6),
        out_specs=(whole,) * 5,
        scratch_shapes=[
            pltpu.VMEM((line, plan.wide, 128), BF16),
            pltpu.VMEM((line, plan.pairs, 128), F32),
            pltpu.VMEM((line, plan.wide, 128), F32),
            pltpu.VMEM((line, plan.spread, 128), F32),
            pltpu.VMEM((line, plan.pairs + plan.half, 128), BF16),
        ],
        compiler_params=params,
        name="direction",
    )(*first, *coarse_all, loads, place, weight, pair_fields, image, flex)
    heard = [message]
    for step in range(1, plan.groups):
        heard.append(swap(message, "grp", step))

    pair_rows = pl.pallas_call(
        functools.partial(local_kernel, plan),
        out_shape=shape(plan.pairs, 256),
        in_specs=[whole] * 4,
        out_specs=whole,
        compiler_params=params,
        name="local",
    )(local_part, schur, place, weight)
    own, *messages = pl.pallas_call(
        functools.partial(coarse_kernel, plan),
        out_shape=(shape(plan.corners, 128),)
        + (shape(plan.third, 128, kind=BF16),) * (line // 2),
        in_specs=[whole] * (plan.groups + 3),
        out_specs=(whole,) * (1 + line // 2),
        compiler_params=params,
        name="coarse",
    )(*heard, missing, first[0], pair_rows)
    last, _ = line_blocks(messages)
    surface_image = pl.pallas_call(
        functools.partial(surface_kernel, plan),
        out_shape=shape(order, 128),
        in_specs=[whole] * 5,
        out_specs=whole,
        compiler_params=params,
        name="surface",
    )(own, schur, coupling_t, weight, local_part)

    solved, preconditioned = pl.pallas_call(
        functools.partial(result_kernel, plan),
        out_shape=(shape(order, 128), shape(order, 128)),
        in_specs=[whole] * (line + 5),
        out_specs=(outside, outside),
        scratch_shapes=[
            pltpu.VMEM((line, plan.wide, 128), BF16),
            pltpu.VMEM((plan.wide, 128), F32),
            pltpu.VMEM((order, 128), F32),
            pltpu.VMEM((order, 128), F32),
            pltpu.SemaphoreType.DMA((2,)),
        ],
        compiler_params=params,
        name="result",
    )(*last, schur_rows, missing, direction, surface_image, pair_fields)
    return solved[None, None], preconditioned[None, None]


def wide_body(
    flexibility,
    dirichlet_schur,
    subdomain_loads,
    coupling,
    coarse_rows,
    neighbors,
    interface_rows,
    coarse_map,
):
    flex_block = flexibility[0, 0]
    schur_block = dirichlet_schur[0, 0]
    loads_block = subdomain_loads[0, 0]
    couple_block = coupling[0, 0]
    coarse_block = coarse_rows[0, 0]
    neighbor_ids = neighbors[0, 0]
    row_lists = interface_rows[0, 0]
    corner_ids = coarse_map[0, 0]
    order_size = flex_block.shape[0]
    column_count = loads_block.shape[1]
    coarse_size = coarse_block.shape[1]
    line_size = lax.axis_size("sub")
    flat_rows = row_lists.reshape(-1)
    destinations = (
        jnp.arange(line_size, dtype=jnp.int32)[:, None] == neighbor_ids[None, :]
    ).astype(jnp.bfloat16)
    pair_mask = jnp.zeros((order_size,), jnp.float32).at[flat_rows].set(1.0)
    weight = (1.0 - 0.5 * pair_mask)[:, None]

    def jump_field(surface):
        picked = surface[flat_rows].reshape(row_lists.shape + (column_count,))
        outgoing = jnp.einsum(
            "dk,kjc->djc", destinations, picked, preferred_element_type=jnp.float32
        ).astype(jnp.bfloat16)
        incoming = lax.all_to_all(outgoing, "sub", split_axis=0, concat_axis=0, tiled=True)
        matched = jnp.einsum(
            "dk,djc->kjc", destinations, incoming, preferred_element_type=jnp.float32
        )
        placed = (
            jnp.zeros((order_size, column_count), jnp.float32)
            .at[flat_rows]
            .set(matched.reshape(-1, column_count))
        )
        return surface.astype(jnp.float32) - placed

    def precondition(residual):
        scaled = (weight * residual).astype(jnp.bfloat16)
        schur_image = jnp.dot(schur_block, scaled, preferred_element_type=jnp.float32).astype(
            jnp.bfloat16
        )
        return weight * jump_field(schur_image)

    def column_dot(first_field, second_field):
        return lax.psum(jnp.sum(weight * first_field * second_field, axis=0), ("sub", "grp"))

    residual = jump_field(loads_block)
    zfield = precondition(residual)
    direction = zfield
    inner = column_dot(residual, zfield)
    dir_half = direction.astype(jnp.bfloat16)
    local_part = jnp.dot(flex_block, dir_half, preferred_element_type=jnp.float32)
    coarse_in = jnp.dot(couple_block.T, dir_half, preferred_element_type=jnp.float32)
    dense_sum = jnp.zeros((coarse_size, column_count), jnp.float32).at[corner_ids].set(coarse_in)
    partial_rows = lax.psum_scatter(dense_sum, "grp", scatter_dimension=0, tiled=True)
    panel_half = lax.psum(partial_rows, "sub").astype(jnp.bfloat16)
    coarse_val = jnp.dot(
        coarse_block,
        lax.all_gather(panel_half, "grp", axis=0, tiled=True),
        preferred_element_type=jnp.float32,
    ).astype(jnp.bfloat16)
    surface = (
        local_part + jnp.dot(couple_block, coarse_val, preferred_element_type=jnp.float32)
    ).astype(jnp.bfloat16)
    operated = jump_field(surface)
    step_size = inner / column_dot(direction, operated)
    solution = step_size * direction
    residual = residual - step_size * operated
    zfield = precondition(residual)
    return (solution[None, None], zfield[None, None])


def body(*arrays):
    flexibility, _, loads, _, coarse_rows, neighbors, interface_rows, _ = arrays
    plan = Plan(
        line=lax.axis_size("sub"),
        groups=lax.axis_size("grp"),
        order=flexibility.shape[2],
        columns=loads.shape[3],
        corners=coarse_rows.shape[2],
        coarse=coarse_rows.shape[3],
        neighbors=neighbors.shape[2],
        each=interface_rows.shape[3],
    )
    if plan.served():
        return line_body(plan, *arrays)
    return wide_body(*arrays)


def solution(mesh):
    placed = (
        P("sub", "grp", None, None),
        P("sub", "grp", None, None),
        P("sub", "grp", None, None),
        P("sub", "grp", None, None),
        P("sub", "grp", None, None),
        P("sub", "grp", None),
        P("sub", "grp", None, None),
        P("sub", "grp", None),
    )
    return jax.shard_map(
        body,
        mesh=mesh,
        in_specs=placed,
        out_specs=(P("sub", "grp", None, None), P("sub", "grp", None, None)),
        check_vma=False,
    )
```
